512 devices in a mesh: ctx: 4 (over y), exp: 128 (over x, z, core).
Axes of the slice: x: 4, y: 4, z: 16, core: 2. Of those that a mesh axis runs over, the one named last changes fastest.
Arguments:
- queries: bfloat16 [256, 32, 2, 2048], P('exp', 'ctx'), may hold values from -20 to 20
- block_keys: bfloat16 [256, 32, 2, 256], P('exp', 'ctx'), may hold values from -6 to 6
- block_values: bfloat16 [256, 32, 2, 256], P('exp', 'ctx'), may hold values from -18 to 18
- cache_keys: bfloat16 [256, 512, 256], P('exp', 'ctx'), may hold values from -6 to 6
- cache_values: bfloat16 [256, 512, 256], P('exp', 'ctx'), may hold values from -18 to 18
- residual: bfloat16 [256, 32, 2, 2048], P('exp', 'ctx'), may hold values from -45 to 45
- out_weight: bfloat16 [2048, 2048], P('ctx'), may hold values from -0.125 to 0.125
- norm_gain: float32 [2048], replicated, may hold values from 0.1 to 1.9
- router: bfloat16 [2048, 128], P(None, 'exp'), may hold values from -0.5 to 0.5
- gate_weight: bfloat16 [128, 2048, 768], P('exp', None, 'ctx'), may hold values from -0.125 to 0.125
- up_weight: bfloat16 [128, 2048, 768], P('exp', None, 'ctx'), may hold values from -0.125 to 0.125
- down_weight: bfloat16 [128, 2048, 768], P('exp', None, 'ctx'), may hold values from -200 to 200
- expert_ids: int32 [256, 32, 2, 8], P('exp', 'ctx'), may hold values from 0 to 127, as said below
Outputs:
- block_output: bfloat16 [256, 32, 2, 2048], P('exp', 'ctx')
The draws below stay inside these ranges and needn't reach their ends.
Inputs may be any that keep to these rules, and one draw needn't show every extreme that they name: `expert_ids`: each row names 8 different experts. Among the 32 rows of rollouts j * 2 to (j + 1) * 2 - 1 at positions m * 8 to (m + 1) * 8 - 1 (both steps), no expert is named by more than 4 rows, and some expert is named by exactly 4 of them.
All inputs are finite; a program needn't handle non-finite values.
Results may differ from the reference program's by a relative error of at most 0.029.
Values may be sent and summed in bfloat16 or wider, within the bound.
A program may use at most 64 MiB of HBM per device.

```python
import jax
import jax.numpy as jnp
from jax import lax

D = 2048
HEADS = 16
KV_HEADS = 2
HEAD_DIM = 128
FF = 768
TOPK = 8
BLOCK = 32
STEPS = 2
ROLL_DEV = 2
EXPERTS = 128
ROLLOUTS = 256
CONTEXT = 512
POS_DEV = 8
TOK_DEV = 32
CAP = 4
N_CTX = 4


def shared_alignment(key):
    base_keys = jax.random.normal(jax.random.fold_in(key, 101), (ROLLOUTS, CONTEXT, KV_HEADS * HEAD_DIM), jnp.float32)
    sign_draw = jax.random.bernoulli(jax.random.fold_in(key, 102), 0.5, (ROLLOUTS, KV_HEADS * HEAD_DIM))
    signs = jnp.where(sign_draw, 1.0, -1.0).astype(jnp.float32)
    strength = 5.0 + 15.0 * jax.random.uniform(jax.random.fold_in(key, 103), (ROLLOUTS,), jnp.float32)
    strength = strength.at[0].set(20.0)
    return (base_keys, signs, strength)


def shared_levels(key):
    sign_draw = jax.random.bernoulli(jax.random.fold_in(key, 111), 0.5, (D,))
    feature_signs = jnp.where(sign_draw, 1.0, -1.0).astype(jnp.float32)
    order = jax.random.permutation(jax.random.fold_in(key, 112), EXPERTS).astype(jnp.float32)
    jitter = jax.random.uniform(jax.random.fold_in(key, 113), (EXPERTS,), jnp.float32)
    levels = -3.0 + 6.0 * (order + jitter) / EXPERTS
    return (feature_signs, levels)


def draw_cache_keys(key, part):
    base_keys, signs, strength = shared_alignment(key)
    values = jnp.clip(base_keys, -6.0, 6.0)
    lowered = 2.0 * HEAD_DIM ** 0.5 / strength
    column_mark = (jnp.arange(KV_HEADS * HEAD_DIM, dtype=jnp.int32) % HEAD_DIM == 0).astype(jnp.float32)
    second_key = signs * (6.0 - lowered[:, None] * column_mark[None, :])
    values = values.at[:, CONTEXT - 1].set(6.0 * signs)
    values = values.at[:, CONTEXT // 2].set(second_key)
    return values.astype(jnp.bfloat16)


def draw_queries(key, part):
    base_keys, signs, strength = shared_alignment(key)
    key = jax.random.fold_in(key, 2)
    values = jnp.clip(jax.random.normal(key, (ROLLOUTS, BLOCK, STEPS, HEADS * HEAD_DIM), jnp.float32), -6.0, 6.0)
    aligned = (strength[:, None] * signs).reshape(ROLLOUTS, KV_HEADS, 1, HEAD_DIM)
    aligned = jnp.broadcast_to(aligned, (ROLLOUTS, KV_HEADS, HEADS // KV_HEADS, HEAD_DIM)).reshape(ROLLOUTS, 1, HEADS * HEAD_DIM)
    values = values.at[:, 0].set(jnp.broadcast_to(aligned, (ROLLOUTS, STEPS, HEADS * HEAD_DIM)))
    return values.astype(jnp.bfloat16)


def draw_residual(key, part):
    feature_signs, levels = shared_levels(key)
    key = jax.random.fold_in(key, 3)
    noise = jnp.clip(jax.random.normal(jax.random.fold_in(key, 1), (ROLLOUTS, BLOCK, STEPS, D), jnp.float32), -5.0, 5.0)
    values = 0.6 * feature_signs + 0.8 * noise
    return values.astype(jnp.bfloat16)


def draw_router(key, part):
    feature_signs, levels = shared_levels(key)
    key = jax.random.fold_in(key, 5)
    spread_part = jnp.clip(jax.random.normal(key, (D, EXPERTS), jnp.float32), -4.0, 4.0) * (0.5 * D ** (-0.5))
    offset_part = -(feature_signs[:, None] * levels[None, :]) / (0.6 * D)
    return (spread_part + offset_part).astype(jnp.bfloat16)


def draw_down_weight(key, part):
    feature_signs, levels = shared_levels(key)
    key = jax.random.fold_in(key, 6)
    values = jnp.clip(jax.random.normal(key, (EXPERTS, D, FF), jnp.float32), -6.0, 6.0) * FF ** (-0.5)
    values = values * (8.0 * jnp.exp(levels))[:, None, None]
    return values.astype(jnp.bfloat16)


def draw_expert_ids(key, part):
    key = jax.random.fold_in(key, 4)
    groups = ROLLOUTS // ROLL_DEV
    shards = BLOCK // POS_DEV
    blocks = groups * shards
    hot = jax.random.randint(jax.random.fold_in(key, 1), (), 0, EXPERTS).astype(jnp.int32)
    expert_range = jnp.arange(EXPERTS, dtype=jnp.int32)
    scores = jax.random.randint(jax.random.fold_in(key, 2), (blocks, EXPERTS), 0, 1 << 20).astype(jnp.int32) * EXPERTS + expert_range
    scores = jnp.where(expert_range[None, :] == hot, 1 << 30, scores)
    ranked = jnp.argsort(scores, axis=1).astype(jnp.int32)
    others = TOK_DEV * TOPK // CAP - 1
    tickets = jnp.concatenate([jnp.full((blocks, CAP), hot, jnp.int32), jnp.repeat(ranked[:, :others], CAP, axis=1)], axis=1)
    grid = tickets.reshape(blocks, TOPK, TOK_DEV).transpose(0, 2, 1)
    row_keys = jax.random.randint(jax.random.fold_in(key, 3), (blocks, TOK_DEV), 0, 1 << 20).astype(jnp.int32) * TOK_DEV + jnp.arange(TOK_DEV, dtype=jnp.int32)
    row_order = jnp.argsort(row_keys, axis=1).astype(jnp.int32)
    grid = jnp.take_along_axis(grid, row_order[:, :, None], axis=1)
    column_keys = jax.random.randint(jax.random.fold_in(key, 4), (blocks, TOPK), 0, 1 << 20).astype(jnp.int32) * TOPK + jnp.arange(TOPK, dtype=jnp.int32)
    column_order = jnp.argsort(column_keys, axis=1).astype(jnp.int32)
    grid = jnp.take_along_axis(grid, column_order[:, None, :], axis=2)
    grid = grid.reshape(groups, shards, ROLL_DEV, POS_DEV, STEPS, TOPK).transpose(0, 2, 1, 3, 4, 5)
    return grid.reshape(ROLLOUTS, BLOCK, STEPS, TOPK).astype(jnp.int32)


def steps_of(rng, extent, cuts, low, top_value):
    loudness = 1.0
    for dim, parts in cuts:
        steps = jax.random.uniform(jax.random.fold_in(jax.random.fold_in(rng, 6), dim), (parts,), jnp.float32, low / len(cuts), top_value / len(cuts))
        loudness = loudness * jnp.repeat(jnp.exp(steps), extent[dim] // parts).reshape((-1,) + (1,) * (len(extent) - 1 - dim))
    return loudness


def centred(own_key, extent, deviation, reach, split=(), held_as=jnp.bfloat16):
    values = jax.random.normal(own_key, extent, jnp.float32) * deviation
    if len(split) > 0:
        values = steps_of(own_key, extent, split, -0.22, 0.18) * values
    return jnp.clip(values, min=-reach, max=reach).astype(held_as)


def setup_inputs(seed: int = 0) -> dict:
    key_of = jax.random.split(jax.random.key(seed), 14)
    return {
        "queries": draw_queries(jax.random.fold_in(key_of[13], 71), 0),
        "block_keys": centred(key_of[1], (ROLLOUTS, BLOCK, STEPS, KV_HEADS * HEAD_DIM), 1.0, 6.0, ((0, 128), (1, 4))),
        "block_values": centred(key_of[2], (ROLLOUTS, BLOCK, STEPS, KV_HEADS * HEAD_DIM), 3.0, 18.0, ((0, 128), (1, 4))),
        "cache_keys": draw_cache_keys(jax.random.fold_in(key_of[13], 71), 0),
        "cache_values": centred(key_of[4], (ROLLOUTS, CONTEXT, KV_HEADS * HEAD_DIM), 3.0, 18.0, ((0, 128), (1, 4))),
        "residual": draw_residual(jax.random.fold_in(key_of[13], 71), 0),
        "out_weight": centred(key_of[6], (HEADS * HEAD_DIM, D), (HEADS * HEAD_DIM) ** -0.5, 0.125, ((0, 4),)),
        "norm_gain": jnp.clip(1.0 + 0.18 * jax.random.normal(key_of[7], (D,), jnp.float32), 0.1, 1.9),
        "router": draw_router(jax.random.fold_in(key_of[13], 71), 0),
        "gate_weight": centred(key_of[9], (EXPERTS, D, FF), D ** -0.5, 0.125, ((0, 128), (2, 4))),
        "up_weight": centred(key_of[10], (EXPERTS, D, FF), D ** -0.5, 0.125, ((0, 128), (2, 4))),
        "down_weight": draw_down_weight(jax.random.fold_in(key_of[13], 71), 0),
        "expert_ids": draw_expert_ids(jax.random.fold_in(key_of[13], 71), 0),
    }


tile_rows = 128

def round_trip(values):
    return lax.optimization_barrier(values.astype(jnp.bfloat16)).astype(jnp.float32)

def attend_rollout(pieces):
    queries, block_keys, block_values, cache_keys, cache_values = pieces
    group_size = HEADS // KV_HEADS
    score_scale = HEAD_DIM ** (-0.5)
    query_grid = queries.astype(jnp.float32).reshape(BLOCK, STEPS, KV_HEADS, group_size, HEAD_DIM)
    cache_kgrid = cache_keys.astype(jnp.float32).reshape(CONTEXT, KV_HEADS, HEAD_DIM)
    cache_vgrid = cache_values.astype(jnp.float32).reshape(CONTEXT, KV_HEADS, HEAD_DIM)
    block_kgrid = block_keys.astype(jnp.float32).reshape(BLOCK, STEPS, KV_HEADS, HEAD_DIM)
    block_vgrid = block_values.astype(jnp.float32).reshape(BLOCK, STEPS, KV_HEADS, HEAD_DIM)
    far_scores = jnp.einsum('psgih,jgh->psgij', query_grid, cache_kgrid) * score_scale
    near_scores = jnp.einsum('psgih,qsgh->psgiq', query_grid, block_kgrid) * score_scale
    row_top = jnp.maximum(far_scores.max(-1), near_scores.max(-1))
    far_exp = jnp.exp(far_scores - row_top[..., None])
    near_exp = jnp.exp(near_scores - row_top[..., None])
    denominator = far_exp.sum(-1) + near_exp.sum(-1)
    far_weights = round_trip(far_exp)
    near_weights = round_trip(near_exp)
    weighted = jnp.einsum('psgij,jgh->psgih', far_weights, cache_vgrid)
    weighted = weighted + jnp.einsum('psgiq,qsgh->psgih', near_weights, block_vgrid)
    attention = weighted / denominator[..., None]
    return attention.reshape(BLOCK, STEPS, HEADS * HEAD_DIM).astype(jnp.bfloat16)

def expert_output(tokens_in, gate_piece, up_piece, down_piece):
    gate_pre = jnp.dot(tokens_in, gate_piece, preferred_element_type=jnp.float32)
    up_pre = jnp.dot(tokens_in, up_piece, preferred_element_type=jnp.float32)
    activated = (jax.nn.silu(gate_pre) * up_pre).astype(jnp.bfloat16)
    quarter = FF // N_CTX
    combined = jnp.zeros((tokens_in.shape[0], D), jnp.float32)
    for quarter_index in range(N_CTX):
        lower_edge = quarter_index * quarter
        partial_out = lax.dot_general(activated[:, lower_edge:lower_edge + quarter], down_piece[:, lower_edge:lower_edge + quarter], (((1,), (1,)), ((), ())), preferred_element_type=jnp.float32)
        combined = combined + round_trip(partial_out)
    return combined.astype(jnp.bfloat16)

def reference(queries, block_keys, block_values, cache_keys, cache_values, residual, out_weight, norm_gain, router, gate_weight, up_weight, down_weight, expert_ids):
    attention = lax.map(attend_rollout, (queries, block_keys, block_values, cache_keys, cache_values))
    head_sum = jnp.dot(attention.reshape(-1, HEADS * HEAD_DIM), out_weight, preferred_element_type=jnp.float32)
    hidden = residual.astype(jnp.float32).reshape(-1, D) + head_sum
    normed = (hidden * lax.rsqrt(lax.optimization_barrier(jnp.mean(hidden * hidden, -1, keepdims=True)) + 1e-06) * norm_gain.astype(jnp.float32)).astype(jnp.bfloat16)
    token_count = hidden.shape[0]
    id_table = expert_ids.reshape(token_count, TOPK).astype(jnp.int32)
    all_scores = jnp.dot(normed, router, preferred_element_type=jnp.float32)
    picked = round_trip(jnp.take_along_axis(all_scores, id_table, axis=1))
    gate_values = jnp.exp(picked - lax.optimization_barrier(jnp.max(picked, -1, keepdims=True)))
    mix_weight = (gate_values / lax.optimization_barrier(jnp.sum(gate_values, -1, keepdims=True))).reshape(-1)
    flat_ids = id_table.reshape(-1)
    assigned = flat_ids.shape[0]
    counts = jax.ops.segment_sum(jnp.ones_like(flat_ids), flat_ids, EXPERTS).astype(jnp.int32)
    starts = (jnp.cumsum(counts) - counts).astype(jnp.int32)
    padded = ((counts + tile_rows - 1) // tile_rows * tile_rows).astype(jnp.int32)
    padded_end = jnp.cumsum(padded).astype(jnp.int32)
    padded_start = padded_end - padded
    sorted_order = jnp.argsort(flat_ids, stable=True).astype(jnp.int32)
    owner_token = (jnp.arange(assigned, dtype=jnp.int32) // TOPK).astype(jnp.int32)
    tile_count = (assigned + tile_rows - 1) // tile_rows + EXPERTS

    def tile_step(accumulated, tile_index):
        first_row = tile_index * tile_rows
        expert = jnp.minimum(jnp.sum((padded_end <= first_row).astype(jnp.int32)), EXPERTS - 1).astype(jnp.int32)
        local_rows = first_row - padded_start[expert] + jnp.arange(tile_rows, dtype=jnp.int32)
        live_rows = (local_rows >= 0) & (local_rows < counts[expert])
        position = jnp.clip(starts[expert] + local_rows, 0, assigned - 1).astype(jnp.int32)
        assignment = sorted_order[position]
        tokens_here = owner_token[assignment]
        result = expert_output(normed[tokens_here], gate_weight[expert], up_weight[expert], down_weight[expert])
        scaled = result.astype(jnp.float32) * (mix_weight[assignment] * live_rows.astype(jnp.float32))[:, None]
        return (accumulated.at[tokens_here].add(scaled), None)
    expert_mix, _ = lax.scan(tile_step, jnp.zeros((token_count, D), jnp.float32), jnp.arange(tile_count, dtype=jnp.int32))
    return (hidden + expert_mix).astype(jnp.bfloat16).reshape(residual.shape)
```

```python
import jax
import jax.numpy as jnp
from jax import lax
from jax.experimental import pallas as pl
from jax.experimental.pallas import tpu as pltpu
from jax.sharding import PartitionSpec as P

D = 2048
HEAD_DIM = 128
TOPK = 8


MESH = pl.DeviceIdType.MESH
BF = jnp.bfloat16
F32 = jnp.float32
NT = (((1,), (1,)), ((), ()))
TOK = 32
ZN = 16


def slot_of(direction, distance):
    if distance == 8:
        return 15
    return 2 * distance - 1 + direction


def layer_kernel(
    queries, block_keys, block_values, cache_keys, cache_values, residual, out_weight,
    gain, router, ids, gate, up, down, out,
    q_all, k_all, v_all, bk_all, bv_all, att, ow, psend, precv, hid, rg, rgf, rfull,
    tok, met, swt, sendx, rx, acc, ysend, ry, part, rss, rsr, wb,
    ex_s, ex_r, own_l, p_s, p_r, rz_s, rz_r, rp_s, rp_r,
    tok_s, tok_r, met_s, met_r, x_s, x_r, y_s, y_r, rs_s, rs_r,
    w_s, w_r, v_s, v_r, loc,
):
    y = lax.axis_index("ctx")
    e = lax.axis_index("exp")
    core = lax.rem(e, 2)
    z = lax.rem(e // 2, ZN)
    x = e // 32
    me8 = x * 2 + core

    def at_z(other):
        return (y, x * 32 + other * 2 + core)

    def at_peer(p):
        return (y, (p // 2) * 32 + z * 2 + lax.rem(p, 2))

    z_next = (at_z(lax.rem(z + 1, ZN)), at_z(lax.rem(z + ZN - 1, ZN)))
    def at_y(d):
        return (lax.rem(y + d, 4), e)

    y_next = (at_y(1), at_y(3))

    barrier = pltpu.get_barrier_semaphore()
    for target in z_next + y_next + (at_y(2),):
        pl.semaphore_signal(barrier, inc=1, device_id=target, device_id_type=MESH)
    for d in range(1, 8):
        pl.semaphore_signal(
            barrier, inc=1, device_id=at_peer(lax.rem(me8 + d, 8)), device_id_type=MESH
        )

    weights = (gate, up, down)
    own_copies = []
    for a in range(3):
        copy = pltpu.make_async_copy(weights[a], wb.at[0, pl.ds(192 * a, 192)], loc.at[a])
        copy.start()
        own_copies.append(copy)

    def columns(index, width):
        return pl.ds(pl.multiple_of(index * width, width), width)

    def shares(owner):
        group = owner // 2
        return (
            queries.at[:, columns(owner, 512)],
            cache_keys.at[:, columns(group, 128)],
            cache_values.at[:, columns(group, 128)],
            block_keys.at[:, columns(group, 128)],
            block_values.at[:, columns(group, 128)],
        )

    gathered = (q_all, k_all, v_all, bk_all, bv_all)
    for a, share in enumerate(shares(y)):
        copy = pltpu.make_async_copy(share, gathered[a].at[y], own_l.at[a])
        copy.start()
        own_copies.append(copy)
    copy = pltpu.make_async_copy(out_weight, ow, own_l.at[5])
    copy.start()
    own_copies.append(copy)
    rg[x, z, core] = router[...]

    pl.semaphore_wait(barrier, 12)

    def exchange(d, a):
        owner = lax.rem(y + d, 4)
        return pltpu.make_async_remote_copy(
            src_ref=shares(owner)[a],
            dst_ref=gathered[a].at[y],
            send_sem=ex_s.at[d - 1, a],
            recv_sem=ex_r.at[d - 1, a],
            device_id=at_y(d),
            device_id_type=MESH,
        )

    def exchanged(d, a):
        source = lax.rem(y + 4 - d, 4)
        pltpu.make_async_remote_copy(
            src_ref=gathered[a].at[source],
            dst_ref=gathered[a].at[source],
            send_sem=ex_s.at[d - 1, a],
            recv_sem=ex_r.at[d - 1, a],
            device_id=at_y(d),
            device_id_type=MESH,
        ).wait_recv()

    for d in (2, 1, 3):
        for a in range(5):
            exchange(d, a).start()

    def ring_row(dr, k):
        held = lax.rem(z + (k - 1 if dr else ZN + 1 - k), ZN)
        return pltpu.make_async_remote_copy(
            src_ref=rg.at[x, held, core],
            dst_ref=rg.at[x, held, core],
            send_sem=rz_s.at[dr, k - 1],
            recv_sem=rz_r.at[dr, k - 1],
            device_id=z_next[dr],
            device_id_type=MESH,
        )

    def ring_row_landed(dr, k):
        held = lax.rem(z + (k if dr else ZN - k), ZN)
        pltpu.make_async_remote_copy(
            src_ref=rg.at[x, held, core],
            dst_ref=rg.at[x, held, core],
            send_sem=rz_s.at[dr, k - 1],
            recv_sem=rz_r.at[dr, k - 1],
            device_id=z_next[dr],
            device_id_type=MESH,
        ).wait_recv()

    def router_rows(d, landed_here):
        p = lax.rem(me8 + 8 - d, 8) if landed_here else me8
        return pltpu.make_async_remote_copy(
            src_ref=rg.at[p // 2, :, lax.rem(p, 2)],
            dst_ref=rg.at[p // 2, :, lax.rem(p, 2)],
            send_sem=rp_s.at[d - 1],
            recv_sem=rp_r.at[d - 1],
            device_id=at_peer(lax.rem(me8 + d, 8)),
            device_id_type=MESH,
        )

    w_copy, v_copy = {}, {}
    for dr in range(2):
        for a in range(3):
            for half in range(2):
                w_copy[dr, a, half] = pltpu.make_async_remote_copy(
                    src_ref=weights[a].at[pl.ds(96 * half, 96)],
                    dst_ref=wb.at[1 + dr, pl.ds(192 * a + 96 * half, 96)],
                    send_sem=w_s.at[dr, a, half],
                    recv_sem=w_r.at[dr, a, half],
                    device_id=y_next[dr],
                    device_id_type=MESH,
                )
            rows = pl.ds(192 * a + 96 * dr, 96)
            v_copy[dr, a] = pltpu.make_async_remote_copy(
                src_ref=wb.at[1 + dr, rows],
                dst_ref=wb.at[3, rows],
                send_sem=v_s.at[dr, a],
                recv_sem=v_r.at[dr, a],
                device_id=y_next[dr],
                device_id_type=MESH,
            )
    for a in range(2):
        for dr in range(2):
            w_copy[dr, a, dr].start()

    ring_row(0, 1).start()
    ring_row(1, 1).start()
    for k in range(1, 9):
        for dr in range(2):
            if k < 8 or dr == 0:
                ring_row_landed(dr, k)
                if k < 7 or (k == 7 and dr == 0):
                    ring_row(dr, k + 1).start()
    for d in range(1, 8):
        router_rows(d, False).start()

    for copy in own_copies:
        copy.wait()
    for d in range(1, 4):
        for a in range(5):
            exchanged(d, a)

    key_step = lax.rem(lax.broadcasted_iota(jnp.int32, (256, 64), 1), 2)
    row_step = lax.rem(lax.broadcasted_iota(jnp.int32, (256, 64), 0), 2)
    for r in range(2):
        near, far = slice(16 * r, 16 * r + 16), slice(128 * r, 128 * r + 128)
        q_rows = jnp.concatenate(
            [q_all[m, near, 128 * h : 128 * h + 128] for h in range(4) for m in range(4)], 0
        )
        far_scores = lax.dot_general(
            q_rows, k_all[:, far, :].reshape(512, 128), NT, preferred_element_type=F32
        )
        near_scores = lax.dot_general(
            q_rows, bk_all[:, near, :].reshape(64, 128), NT, preferred_element_type=F32
        )
        far_scores = far_scores * HEAD_DIM ** (-0.5)
        near_scores = jnp.where(
            key_step == row_step, near_scores * HEAD_DIM ** (-0.5), -3e38
        )
        row_top = jnp.maximum(
            jnp.max(far_scores, -1, keepdims=True), jnp.max(near_scores, -1, keepdims=True)
        )
        far_exp = jnp.exp(far_scores - row_top)
        near_exp = jnp.where(key_step == row_step, jnp.exp(near_scores - row_top), 0.0)
        total = jnp.sum(far_exp, -1, keepdims=True) + jnp.sum(near_exp, -1, keepdims=True)
        weighted = jnp.dot(
            far_exp.astype(BF), v_all[:, far, :].reshape(512, 128), preferred_element_type=F32
        ) + jnp.dot(
            near_exp.astype(BF), bv_all[:, near, :].reshape(64, 128), preferred_element_type=F32
        )
        attended = (weighted / total).astype(BF)
        for h in range(4):
            for m in range(4):
                att[m, near, 128 * h : 128 * h + 128] = attended[
                    64 * h + 16 * m : 64 * h + 16 * m + 16
                ]

    for c in range(4):
        cols = slice(512 * c, 512 * c + 512)
        projected = jnp.dot(
            att[...].reshape(128, 512), ow[:, cols], preferred_element_type=F32
        ).reshape(4, TOK, 512)
        part[0:4, :, cols] = projected
        psend[:, :, cols] = projected.astype(BF)

    p_copy = []
    for d in (2, 1, 3):
        p_copy.append(
            pltpu.make_async_remote_copy(
                src_ref=psend.at[lax.rem(y + d, 4)],
                dst_ref=precv.at[d - 1],
                send_sem=p_s.at[d - 1],
                recv_sem=p_r.at[d - 1],
                device_id=at_y(d),
                device_id_type=MESH,
            )
        )
        p_copy[-1].start()
    for dr in range(2):
        w_copy[dr, 2, dr].start()
    for a in range(3):
        for dr in range(2):
            w_copy[dr, a, 1 - dr].start()

    for d in range(1, 8):
        router_rows(d, True).wait_recv()
    rgf[...] = rg[...].reshape(2048, 128).astype(F32)
    for k in range(16):
        rfull[:, 128 * k : 128 * k + 128] = rgf[pl.ds(k, 128, stride=16), :].astype(BF)

    for copy in p_copy:
        copy.wait_recv()
    hidden = residual[...].astype(F32) + part[y]
    for d in range(3):
        hidden = hidden + precv[d].astype(F32)
    hid[...] = hidden
    scale = lax.rsqrt(jnp.mean(hidden * hidden, -1, keepdims=True) + 1e-06)
    normed = (hidden * scale * gain[...]).astype(BF)
    tok[0] = normed
    scores = lax.dot_general(rfull[...], normed, NT, preferred_element_type=F32)
    scores = scores.astype(BF).astype(F32)
    expert_row = lax.broadcasted_iota(jnp.int32, (128, TOK), 0)
    named = expert_row == ids[0:1, :]
    for k in range(1, 8):
        named = named | (expert_row == ids[k : k + 1, :])
    hits = jnp.where(named, 1.0, 0.0)
    top = jnp.max(jnp.where(named, scores, -3e38), 0, keepdims=True)
    grown = jnp.where(named, jnp.exp(jnp.minimum(scores - top, 0.0)), 0.0)
    mix = grown / jnp.sum(grown, 0, keepdims=True)
    before = lax.broadcasted_iota(jnp.int32, (TOK, TOK), 0) < lax.broadcasted_iota(
        jnp.int32, (TOK, TOK), 1
    )
    rank = jnp.dot(
        hits.astype(BF), jnp.where(before, 1.0, 0.0).astype(BF), preferred_element_type=F32
    )
    code = jnp.where(named, 2.0 * rank + mix, -1.0)
    for k in range(4):
        met[0, :, 32 * k : 32 * k + 32] = code[32 * k : 32 * k + 32, :]

    tok_copy, met_copy = {}, {}
    for dr in range(2):
        for k in range(1, 9):
            src = 0 if k == 1 else slot_of(dr, k - 1)
            dst = slot_of(dr, k)
            for half in range(2):
                if k == 8 and half != dr:
                    continue
                rows = pl.ds(16 * half, 16)
                tok_copy[dr, k, half] = pltpu.make_async_remote_copy(
                    src_ref=tok.at[src, rows],
                    dst_ref=tok.at[dst, rows],
                    send_sem=tok_s.at[dr, k - 1, half],
                    recv_sem=tok_r.at[dr, k - 1, half],
                    device_id=z_next[dr],
                    device_id_type=MESH,
                )
            if k < 8 or dr == 0:
                met_copy[dr, k] = pltpu.make_async_remote_copy(
                    src_ref=met.at[src],
                    dst_ref=met.at[dst],
                    send_sem=met_s.at[dr, k - 1],
                    recv_sem=met_r.at[dr, k - 1],
                    device_id=z_next[dr],
                    device_id_type=MESH,
                )

    for dr in range(2):
        met_copy[dr, 1].start()
        tok_copy[dr, 1, 0].start()
        tok_copy[dr, 1, 1].start()

    row = lax.broadcasted_iota(jnp.int32, (128, 128), 0)
    lane = lax.broadcasted_iota(jnp.int32, (128, 128), 1)
    row_x, row_c = row // 32, lax.rem(row // 16, 2)
    row_q, row_s = lax.rem(row // 4, 4), lax.rem(row, 4)
    lane_g = lane // 32

    def folded(values):
        total = values
        for k in range(1, 4):
            total = total + pltpu.roll(values, 32 * k, 1)
        return jnp.where(lane_g == row_q, total, 0.0)

    def x_copy(g, d):
        p = lax.rem(me8 + d, 8)
        return pltpu.make_async_remote_copy(
            src_ref=sendx.at[g, p],
            dst_ref=rx.at[g, me8],
            send_sem=x_s.at[g, d - 1],
            recv_sem=x_r.at[g, d - 1],
            device_id=at_peer(p),
            device_id_type=MESH,
        )

    def y_copy(g, d):
        p = lax.rem(me8 + d, 8)
        return pltpu.make_async_remote_copy(
            src_ref=ysend.at[g, p],
            dst_ref=ry.at[g, me8],
            send_sem=y_s.at[g, d - 1],
            recv_sem=y_r.at[g, d - 1],
            device_id=at_peer(p),
            device_id_type=MESH,
        )

    def landed(buffer, sems, g, d):
        p = lax.rem(me8 + 8 - d, 8)
        pltpu.make_async_remote_copy(
            src_ref=buffer.at[g, p],
            dst_ref=buffer.at[g, p],
            send_sem=sems.at[g, d - 1],
            recv_sem=sems.at[g, d - 1],
            device_id=at_peer(p),
            device_id_type=MESH,
        ).wait_recv()

    def dispatch(g):
        value = jnp.full((128, 128), -1.0, F32)
        for q in range(4):
            for c in range(2):
                line = met[4 * g + q, pl.ds(2 * z + c, 1), :]
                value = jnp.where((row_q == q) & (row_c == c), line, value)
        rank_here = (
            jnp.where(value >= 2.0, 1.0, 0.0)
            + jnp.where(value >= 4.0, 1.0, 0.0)
            + jnp.where(value >= 6.0, 1.0, 0.0)
        )
        picked = (value >= 0.0) & (lane_g == row_x) & (rank_here == row_s.astype(F32))
        choose = folded(jnp.where(picked, 1.0, 0.0)).astype(BF)
        weigh = folded(jnp.where(picked, value - 2.0 * rank_here, 0.0))
        swt[g] = weigh.T.astype(BF)
        for c in range(4):
            cols = slice(512 * c, 512 * c + 512)
            rows = tok[4 * g : 4 * g + 4, :, cols].reshape(128, 512)
            sent = jnp.dot(choose, rows, preferred_element_type=F32).astype(BF)
            sendx[g, :, :, cols] = sent.reshape(8, 16, 512)
        for d in range(1, 8):
            x_copy(g, d).start()
        rx[g, me8] = sendx[g, me8]

    for k in range(1, 9):
        for half in range(2):
            for dr in range(2):
                if half == 0 and (dr, k) in met_copy:
                    met_copy[dr, k].wait_recv()
                    if (dr, k + 1) in met_copy:
                        met_copy[dr, k + 1].start()
                if (dr, k, half) in tok_copy:
                    tok_copy[dr, k, half].wait_recv()
                    if (dr, k + 1, half) in tok_copy:
                        tok_copy[dr, k + 1, half].start()
        if k % 2 == 0:
            dispatch(k // 2 - 1)
        if k in (2, 4, 6):
            for dr in range(2):
                w_copy[dr, k // 2 - 1, dr].wait_recv()
                v_copy[dr, k // 2 - 1].start()

    for g in range(4):
        for d in range(1, 8):
            landed(rx, x_r, g, d)

    def hidden_units(slot, rows):
        gate_pre = lax.dot_general(rows, wb[slot, 0:192], NT, preferred_element_type=F32)
        up_pre = lax.dot_general(rows, wb[slot, 192:384], NT, preferred_element_type=F32)
        return (gate_pre * (1.0 / (1.0 + jnp.exp(-gate_pre))) * up_pre).astype(BF)

    def quarter(slot):
        def body(h, carry):
            act = hidden_units(slot, rx[pl.ds(2 * h, 2)].reshape(256, D))
            for c in range(4):
                cols = slice(512 * c, 512 * c + 512)
                part_out = jnp.dot(act, wb[slot, 384:576, cols], preferred_element_type=F32)
                if slot == 0:
                    acc[pl.ds(2 * h, 2), :, cols] = part_out.reshape(2, 128, 512)
                else:
                    acc[pl.ds(2 * h, 2), :, cols] += part_out.reshape(2, 128, 512)
            return carry

        lax.fori_loop(0, 2, body, 0)

    quarter(0)
    for dr in range(2):
        for a in range(3):
            w_copy[dr, a, 1 - dr].wait_recv()
        quarter(1 + dr)
    for dr in range(2):
        for a in range(3):
            v_copy[dr, a].wait_recv()

    def last_quarter(g):
        act = hidden_units(3, rx[g].reshape(128, D))
        for c in range(4):
            cols = slice(512 * c, 512 * c + 512)
            part_out = jnp.dot(act, wb[3, 384:576, cols], preferred_element_type=F32)
            ysend[g, :, :, cols] = (acc[g, :, cols] + part_out).astype(BF).reshape(8, 16, 512)
        for d in range(1, 8):
            y_copy(g, d).start()
        ry[g, me8] = ysend[g, me8]

    for g in (3, 2, 1, 0):
        last_quarter(g)

    def gather_back(g):
        for d in range(1, 8):
            landed(ry, y_r, g, d)
        for c in range(4):
            cols = slice(512 * c, 512 * c + 512)
            rows = ry[g, :, :, cols].reshape(128, 512)
            mixed = jnp.dot(swt[g], rows, preferred_element_type=F32)
            part[4 * g : 4 * g + 4, :, cols] = mixed.reshape(4, 32, 512)

    rs_copy = {}
    for dr in range(2):
        for j in range(8):
            for half in range(2):
                if j == 0 and half != dr:
                    continue
                rows = pl.ds(16 * half, 16)
                rs_copy[dr, j, half] = pltpu.make_async_remote_copy(
                    src_ref=rss.at[dr, j, rows],
                    dst_ref=rsr.at[dr, j, rows],
                    send_sem=rs_s.at[dr, j, half],
                    recv_sem=rs_r.at[dr, j, half],
                    device_id=z_next[dr],
                    device_id_type=MESH,
                )

    gather_back(3)
    for j in range(8):
        distance = 8 - j
        if j in (2, 4, 6):
            gather_back(3 - j // 2)
        for half in range(2):
            rows = slice(16 * half, 16 * half + 16)
            for dr in range(2):
                if (dr, j, half) not in rs_copy:
                    continue
                source = slot_of(1 - dr, distance)
                total = part[source, rows, :]
                if (dr, j - 1, half) in rs_copy:
                    rs_copy[dr, j - 1, half].wait_recv()
                    total = total + rsr[dr, j - 1, rows, :].astype(F32)
                rss[dr, j, rows, :] = total.astype(BF)
                rs_copy[dr, j, half].start()
    for half in range(2):
        rows = slice(16 * half, 16 * half + 16)
        total = hid[rows, :] + part[0, rows, :]
        for dr in range(2):
            rs_copy[dr, 7, half].wait_recv()
            total = total + rsr[dr, 7, rows, :].astype(F32)
        out[rows, :] = total.astype(BF)

    for group in (tok_copy, met_copy, w_copy, v_copy, rs_copy):
        for copy in group.values():
            copy.wait_send()
    for copy in p_copy:
        copy.wait_send()
    for d in range(1, 4):
        for a in range(5):
            exchange(d, a).wait_send()
    for k in range(1, 9):
        for dr in range(2):
            if k < 8 or dr == 0:
                ring_row(dr, k).wait_send()
    for d in range(1, 8):
        router_rows(d, False).wait_send()
    for g in range(4):
        for d in range(1, 8):
            x_copy(g, d).wait_send()
            y_copy(g, d).wait_send()


def layer(*operands):
    vmem = pl.BlockSpec(memory_space=pltpu.VMEM)
    anywhere = pl.BlockSpec(memory_space=pl.ANY)
    dma = pltpu.SemaphoreType.DMA
    return pl.pallas_call(
        layer_kernel,
        out_shape=jax.ShapeDtypeStruct((TOK, D), BF),
        in_specs=[anywhere] * 5 + [vmem, anywhere] + [vmem] * 3 + [anywhere] * 3,
        out_specs=vmem,
        scratch_shapes=[
            pltpu.VMEM((4, TOK, 512), BF),
            pltpu.VMEM((4, 256, 128), BF),
            pltpu.VMEM((4, 256, 128), BF),
            pltpu.VMEM((4, TOK, 128), BF),
            pltpu.VMEM((4, TOK, 128), BF),
            pltpu.VMEM((4, TOK, 512), BF),
            pltpu.VMEM((512, D), BF),
            pltpu.VMEM((4, TOK, D), BF),
            pltpu.VMEM((3, TOK, D), BF),
            pltpu.VMEM((TOK, D), F32),
            pltpu.VMEM((4, ZN, 2, 16, 128), BF),
            pltpu.VMEM((2048, 128), F32),
            pltpu.VMEM((128, D), BF),
            pltpu.VMEM((16, TOK, D), BF),
            pltpu.VMEM((16, TOK, 128), F32),
            pltpu.VMEM((4, 128, 128), BF),
            pltpu.VMEM((4, 8, 16, D), BF),
            pltpu.VMEM((4, 8, 16, D), BF),
            pltpu.VMEM((4, 128, D), F32),
            pltpu.VMEM((4, 8, 16, D), BF),
            pltpu.VMEM((4, 8, 16, D), BF),
            pltpu.VMEM((16, TOK, D), F32),
            pltpu.VMEM((2, 8, TOK, D), BF),
            pltpu.VMEM((2, 8, TOK, D), BF),
            pltpu.VMEM((4, 576, D), BF),
            dma((3, 5)), dma((3, 5)), dma((6,)),
            dma((3,)), dma((3,)),
            dma((2, 8)), dma((2, 8)),
            dma((7,)), dma((7,)),
            dma((2, 8, 2)), dma((2, 8, 2)),
            dma((2, 8)), dma((2, 8)),
            dma((4, 7)), dma((4, 7)),
            dma((4, 7)), dma((4, 7)),
            dma((2, 8, 2)), dma((2, 8, 2)),
            dma((2, 3, 2)), dma((2, 3, 2)),
            dma((2, 3)), dma((2, 3)),
            dma((3,)),
        ],
        compiler_params=pltpu.CompilerParams(
            collective_id=0, has_side_effects=True, vmem_limit_bytes=56 * 1024 * 1024
        ),
        cost_estimate=pl.CostEstimate(
            flops=2 * 3 * 512 * 2048 * 768, bytes_accessed=8 << 20, transcendentals=512 * 768
        ),
    )(*operands)


def per_device(
    queries,
    block_keys,
    block_values,
    cache_keys,
    cache_values,
    residual,
    out_weight,
    norm_gain,
    router,
    gate_weight,
    up_weight,
    down_weight,
    expert_ids,
):
    block_output = layer(
        queries.reshape(TOK, D),
        block_keys.reshape(TOK, 256),
        block_values.reshape(TOK, 256),
        cache_keys.reshape(256, 256),
        cache_values.reshape(256, 256),
        residual.reshape(TOK, D),
        out_weight,
        norm_gain.reshape(1, D),
        router.reshape(16, 128),
        expert_ids.reshape(TOK, TOPK).T,
        gate_weight[0].T,
        up_weight[0].T,
        down_weight[0].T,
    )
    return block_output.reshape(residual.shape)


def solution(mesh):
    in_specs = (
        P("exp", "ctx", None, None),
        P("exp", "ctx", None, None),
        P("exp", "ctx", None, None),
        P("exp", "ctx", None),
        P("exp", "ctx", None),
        P("exp", "ctx", None, None),
        P("ctx", None),
        P(),
        P(None, "exp"),
        P("exp", None, "ctx"),
        P("exp", None, "ctx"),
        P("exp", None, "ctx"),
        P("exp", "ctx", None, None),
    )
    out_specs = P("exp", "ctx", None, None)
    return jax.shard_map(
        per_device, mesh=mesh, in_specs=in_specs, out_specs=out_specs, check_vma=False
    )
```

```python
import functools

import jax
import jax.numpy as jnp
from jax import lax
from jax.experimental import pallas as pl
from jax.experimental.pallas import tpu as pltpu
from jax.sharding import PartitionSpec as P

D = 2048
HEAD_DIM = 128
TOPK = 8


MESH = pl.DeviceIdType.MESH
BF = jnp.bfloat16
F32 = jnp.float32
NT = (((1,), (1,)), ((), ()))
TOK = 32
ZN = 16


def slot_of(direction, distance):
    if distance == 8:
        return 15
    return 2 * distance - 1 + direction


def layer_kernel(
    q_in, bk_in, bv_in, cache_keys, cache_values, residual, out_weight,
    gain, router, ids, gate, up, down, out,
    queries, block_keys, block_values, q_all, k_all, v_all, bk_all, bv_all, att, ow, psend, precv, hid, rt, rg, rgf, rfull,
    tok, met, swt, sendx, rx, act, ysend, ry, part, rss, rsr, wb,
    ex_s, ex_r, own_l, p_s, p_r, rz_s, rz_r, rp_s, rp_r,
    tok_s, tok_r, met_s, met_r, x_s, x_r, y_s, y_r, rs_s, rs_r,
    w_s, w_r, v_s, v_r, o_s, o_r, loc,
):
    y = lax.axis_index("ctx")
    e = lax.axis_index("exp")
    core = lax.rem(e, 2)
    z = lax.rem(e // 2, ZN)
    x = e // 32
    me8 = x * 2 + core

    def at_z(other):
        return (y, x * 32 + other * 2 + core)

    def at_peer(p):
        return (y, (p // 2) * 32 + z * 2 + lax.rem(p, 2))

    def at_slot(p):
        kept = lax.rem(p, 2)
        return (lax.rem(y + kept * (1 + 2 * core), 4), (p // 2) * 32 + z * 2 + kept)

    def at_source(p):
        other = lax.rem(p, 2)
        return (lax.rem(y + core * (3 - 2 * other), 4), (p // 2) * 32 + z * 2 + other)

    def at_line(d, c):
        return (lax.rem(y + d, 4), x * 32 + z * 2 + c)

    def at_y(d):
        return at_line(d, core)

    def at_across(d, k, c):
        return (lax.rem(y + d, 4), lax.rem(x + k, 4) * 32 + z * 2 + c)

    z_next = (at_z(lax.rem(z + 1, ZN)), at_z(lax.rem(z + ZN - 1, ZN)))
    sibling = at_line(0, 1 - core)
    keeper = core == lax.rem(y, 2)

    pending = []

    def go(copy):
        copy.start()
        pending.append(copy)
        return copy

    barrier = pltpu.get_barrier_semaphore()

    def greet(target):
        pl.semaphore_signal(barrier, inc=1, device_id=target, device_id_type=MESH)

    for d in range(1, ZN):
        greet(at_z(lax.rem(z + d, ZN)))
    for d in range(1, 8):
        greet(at_peer(lax.rem(me8 + d, 8)))
    for d in range(1, 4):
        for c in range(2):
            greet(at_line(d, c))

    @pl.when(core == 0)
    def _():
        for k in range(1, 4):
            greet(at_across(1, k, 1))

    @pl.when(core == 1)
    def _():
        for k in range(1, 4):
            greet(at_across(3, k, 0))
            greet(at_across(3, k, 1))
            greet(at_across(1, k, 1))

    weights = (gate, up, down)
    own_copies = []

    def own_weight(a):
        return pltpu.make_async_copy(weights[a], wb.at[0, pl.ds(192 * a, 192)], loc.at[a])

    @pl.when(keeper)
    def _():
        for a in range(3):
            own_weight(a).start()

    queries[...] = q_in[...].reshape(TOK, D)
    block_keys[...] = bk_in[...].reshape(TOK, 256)
    block_values[...] = bv_in[...].reshape(TOK, 256)
    for k in range(16):
        rt[k : k + 1, :] = router[0:1, 128 * k : 128 * k + 128].astype(F32)
    rg[x, z, core] = rt[...].astype(BF)

    def columns(index, width):
        return pl.ds(pl.multiple_of(index * width, width), width)

    def shares(owner):
        group = owner // 2
        return (
            queries.at[:, columns(owner, 512)],
            cache_keys.at[:, columns(group, 128)],
            cache_values.at[:, columns(group, 128)],
            block_keys.at[:, columns(group, 128)],
            block_values.at[:, columns(group, 128)],
        )

    gathered = (q_all, k_all, v_all, bk_all, bv_all)
    for a, share in enumerate(shares(y)):
        copy = pltpu.make_async_copy(share, gathered[a].at[y], own_l.at[a])
        copy.start()
        own_copies.append(copy)
    copy = pltpu.make_async_copy(out_weight, ow, own_l.at[5])
    copy.start()
    own_copies.append(copy)

    pl.semaphore_wait(barrier, 31 + 6 * core)

    def exchange(d, a):
        owner = lax.rem(y + d, 4)
        return pltpu.make_async_remote_copy(
            src_ref=shares(owner)[a],
            dst_ref=gathered[a].at[y],
            send_sem=ex_s.at[d - 1, a],
            recv_sem=ex_r.at[d - 1, a],
            device_id=at_y(d),
            device_id_type=MESH,
        )

    def exchanged(d, a):
        source = lax.rem(y + 4 - d, 4)
        pltpu.make_async_remote_copy(
            src_ref=gathered[a].at[source],
            dst_ref=gathered[a].at[source],
            send_sem=ex_s.at[d - 1, a],
            recv_sem=ex_r.at[d - 1, a],
            device_id=at_y(d),
            device_id_type=MESH,
        ).wait_recv()

    for d in (2, 1, 3):
        for a in range(5):
            go(exchange(d, a))

    def router_row(d, landed_here):
        held = lax.rem(z + ZN - d, ZN) if landed_here else z
        return pltpu.make_async_remote_copy(
            src_ref=rg.at[x, held, core],
            dst_ref=rg.at[x, held, core],
            send_sem=rz_s.at[d - 1],
            recv_sem=rz_r.at[d - 1],
            device_id=at_z(lax.rem(z + d, ZN)),
            device_id_type=MESH,
        )

    def router_rows(d, landed_here):
        p = lax.rem(me8 + 8 - d, 8) if landed_here else me8
        return pltpu.make_async_remote_copy(
            src_ref=rg.at[p // 2, :, lax.rem(p, 2)],
            dst_ref=rg.at[p // 2, :, lax.rem(p, 2)],
            send_sem=rp_s.at[d - 1],
            recv_sem=rp_r.at[d - 1],
            device_id=at_peer(lax.rem(me8 + d, 8)),
            device_id_type=MESH,
        )

    pieces = ((0, 32), (32, 64))

    def give(dr, a, half, piece):
        start, count = pieces[piece]
        rows = pl.ds(192 * a + 96 * half + start, count)
        return pltpu.make_async_remote_copy(
            src_ref=weights[a].at[pl.ds(96 * half + start, count)],
            dst_ref=wb.at[1 + dr, rows],
            send_sem=w_s.at[dr, a, half, piece],
            recv_sem=w_r.at[dr, a, piece],
            device_id=at_line((1, 3, 2)[dr], half),
            device_id_type=MESH,
        )

    def share_weight(a):
        return pltpu.make_async_remote_copy(
            src_ref=weights[a],
            dst_ref=wb.at[0, pl.ds(192 * a, 192)],
            send_sem=o_s.at[a],
            recv_sem=o_r.at[a],
            device_id=sibling,
            device_id_type=MESH,
        )

    def send_weights(a, piece):
        @pl.when(keeper)
        def _():
            for half in range(2):
                give(2, a, half, piece).start()
            if piece == 1:
                share_weight(a).start()

        @pl.when(jnp.logical_not(keeper))
        def _():
            for half in range(2):
                give(0, a, half, piece).start()
                give(1, a, half, piece).start()

    def given(slot, a, piece):
        start, count = pieces[piece]
        rows = pl.ds(pl.multiple_of(192 * a + 96 * core + start, 32), count)
        pltpu.make_async_remote_copy(
            src_ref=wb.at[slot, rows],
            dst_ref=wb.at[slot, rows],
            send_sem=v_s.at[slot - 1, a],
            recv_sem=w_r.at[slot - 1, a, piece],
            device_id=sibling,
            device_id_type=MESH,
        ).wait_recv()

    def half_copy(slot, a, half):
        rows = pl.ds(pl.multiple_of(192 * a + 96 * half, 32), 96)
        return pltpu.make_async_remote_copy(
            src_ref=wb.at[slot, rows],
            dst_ref=wb.at[slot, rows],
            send_sem=v_s.at[slot - 1, a],
            recv_sem=v_r.at[slot - 1, a],
            device_id=sibling,
            device_id_type=MESH,
        )

    def pass_on(a):
        for slot in range(1, 4):
            for piece in range(2):
                given(slot, a, piece)
            go(half_copy(slot, a, core))

    def weight_ready(a):
        for slot in range(1, 4):
            half_copy(slot, a, 1 - core).wait_recv()

        @pl.when(keeper)
        def _():
            own_weight(a).wait()

        @pl.when(jnp.logical_not(keeper))
        def _():
            share_weight(a).wait_recv()

    for d in range(1, ZN):
        go(router_row(d, False))
    send_weights(0, 0)
    for d in range(1, ZN):
        router_row(d, True).wait_recv()
    for d in range(1, 8):
        go(router_rows(d, False))

    for copy in own_copies:
        copy.wait()
    for d in range(1, 4):
        for a in range(5):
            exchanged(d, a)

    key_step = lax.rem(lax.broadcasted_iota(jnp.int32, (256, 64), 1), 2)
    row_step = lax.rem(lax.broadcasted_iota(jnp.int32, (256, 64), 0), 2)
    for r in range(2):
        near, far = slice(16 * r, 16 * r + 16), slice(128 * r, 128 * r + 128)
        q_rows = jnp.concatenate(
            [q_all[m, near, 128 * h : 128 * h + 128] for h in range(4) for m in range(4)], 0
        )
        far_scores = lax.dot_general(
            q_rows, k_all[:, far, :].reshape(512, 128), NT, preferred_element_type=F32
        )
        near_scores = lax.dot_general(
            q_rows, bk_all[:, near, :].reshape(64, 128), NT, preferred_element_type=F32
        )
        far_scores = far_scores * HEAD_DIM ** (-0.5)
        near_scores = jnp.where(
            key_step == row_step, near_scores * HEAD_DIM ** (-0.5), -3e38
        )
        row_top = jnp.maximum(
            jnp.max(far_scores, -1, keepdims=True), jnp.max(near_scores, -1, keepdims=True)
        )
        far_exp = jnp.exp(far_scores - row_top)
        near_exp = jnp.where(key_step == row_step, jnp.exp(near_scores - row_top), 0.0)
        total = jnp.sum(far_exp, -1, keepdims=True) + jnp.sum(near_exp, -1, keepdims=True)
        weighted = jnp.dot(
            far_exp.astype(BF), v_all[:, far, :].reshape(512, 128), preferred_element_type=F32
        ) + jnp.dot(
            near_exp.astype(BF), bv_all[:, near, :].reshape(64, 128), preferred_element_type=F32
        )
        attended = (weighted / total).astype(BF)
        for h in range(4):
            for m in range(4):
                att[m, near, 128 * h : 128 * h + 128] = attended[
                    64 * h + 16 * m : 64 * h + 16 * m + 16
                ]

    for c in range(4):
        cols = slice(512 * c, 512 * c + 512)
        projected = jnp.dot(
            att[...].reshape(128, 512), ow[:, cols], preferred_element_type=F32
        ).reshape(4, TOK, 512)
        part[0:4, :, cols] = projected
        psend[:, :, cols] = projected.astype(BF)

    p_copy = []
    for d in (2, 1, 3):
        p_copy.append(
            pltpu.make_async_remote_copy(
                src_ref=psend.at[lax.rem(y + d, 4)],
                dst_ref=precv.at[d - 1],
                send_sem=p_s.at[d - 1],
                recv_sem=p_r.at[d - 1],
                device_id=at_y(d),
                device_id_type=MESH,
            )
        )
        go(p_copy[-1])
    send_weights(0, 1)
    send_weights(1, 0)
    send_weights(1, 1)

    for d in range(1, 8):
        router_rows(d, True).wait_recv()
    rgf[...] = rg[...].reshape(2048, 128).astype(F32)
    for k in range(16):
        rfull[:, 128 * k : 128 * k + 128] = rgf[pl.ds(k, 128, stride=16), :].astype(BF)

    for copy in p_copy:
        copy.wait_recv()
    hidden = residual[...].reshape(TOK, D).astype(F32) + part[y]
    for d in range(3):
        hidden = hidden + precv[d].astype(F32)
    hid[...] = hidden
    scale = lax.rsqrt(jnp.mean(hidden * hidden, -1, keepdims=True) + 1e-06)
    normed = (hidden * scale * gain[...]).astype(BF)
    tok[0] = normed
    scores = lax.dot_general(rfull[...], normed, NT, preferred_element_type=F32)
    scores = scores.astype(BF).astype(F32)
    id_rows = ids[...].reshape(TOK, TOPK)
    expert_lane = lax.broadcasted_iota(jnp.int32, (TOK, 128), 1)
    named = expert_lane == id_rows[:, 0:1]
    for k in range(1, TOPK):
        named = named | (expert_lane == id_rows[:, k : k + 1])
    hits = jnp.where(named, 1.0, 0.0).T
    named = hits > 0.0
    top = jnp.max(jnp.where(named, scores, -3e38), 0, keepdims=True)
    grown = jnp.where(named, jnp.exp(jnp.minimum(scores - top, 0.0)), 0.0)
    mix = grown / jnp.sum(grown, 0, keepdims=True)
    before = lax.broadcasted_iota(jnp.int32, (TOK, TOK), 0) < lax.broadcasted_iota(
        jnp.int32, (TOK, TOK), 1
    )
    rank = jnp.dot(
        hits.astype(BF), jnp.where(before, 1.0, 0.0).astype(BF), preferred_element_type=F32
    )
    code = jnp.where(named, 2.0 * rank + mix, -1.0)
    for k in range(4):
        met[0, :, 32 * k : 32 * k + 32] = code[32 * k : 32 * k + 32, :]

    tok_copy, met_copy = {}, {}
    for dr in range(2):
        for k in range(1, 9):
            src = 0 if k == 1 else slot_of(dr, k - 1)
            dst = slot_of(dr, k)
            for chunk in range(4):
                if k == 8 and chunk // 2 != dr:
                    continue
                rows, cols = pl.ds(16 * (chunk // 2), 16), pl.ds(1024 * (chunk % 2), 1024)
                tok_copy[dr, k, chunk] = pltpu.make_async_remote_copy(
                    src_ref=tok.at[src, rows, cols],
                    dst_ref=tok.at[dst, rows, cols],
                    send_sem=tok_s.at[dr, k - 1, chunk],
                    recv_sem=tok_r.at[dr, k - 1, chunk],
                    device_id=z_next[dr],
                    device_id_type=MESH,
                )
            if k < 8 or dr == 0:
                met_copy[dr, k] = pltpu.make_async_remote_copy(
                    src_ref=met.at[src],
                    dst_ref=met.at[dst],
                    send_sem=met_s.at[dr, k - 1],
                    recv_sem=met_r.at[dr, k - 1],
                    device_id=z_next[dr],
                    device_id_type=MESH,
                )

    for dr in range(2):
        go(met_copy[dr, 1])
    for chunk in range(4):
        for dr in range(2):
            go(tok_copy[dr, 1, chunk])
    pass_on(0)

    row = lax.broadcasted_iota(jnp.int32, (128, 128), 0)
    lane = lax.broadcasted_iota(jnp.int32, (128, 128), 1)
    row_x, row_c = row // 32, lax.rem(row // 16, 2)
    row_q, row_s = lax.rem(row // 4, 4), lax.rem(row, 4)
    lane_g = lane // 32

    def folded(values):
        total = values
        for k in range(1, 4):
            total = total + pltpu.roll(values, 32 * k, 1)
        return jnp.where(lane_g == row_q, total, 0.0)

    def x_copy(g, d):
        p = lax.rem(me8 + d, 8)
        return pltpu.make_async_remote_copy(
            src_ref=sendx.at[g, p],
            dst_ref=rx.at[g, me8],
            send_sem=x_s.at[g, d],
            recv_sem=x_r.at[g, d],
            device_id=at_slot(p),
            device_id_type=MESH,
        )

    def y_copy(g, d):
        p = lax.rem(me8 + d, 8)
        return pltpu.make_async_remote_copy(
            src_ref=ysend.at[g, p],
            dst_ref=ry.at[g, me8],
            send_sem=y_s.at[g, d],
            recv_sem=y_r.at[g, d],
            device_id=at_source(p),
            device_id_type=MESH,
        )

    def landed(buffer, sems, g, d):
        p = lax.rem(me8 + 8 - d, 8)
        pltpu.make_async_remote_copy(
            src_ref=buffer.at[g, p],
            dst_ref=buffer.at[g, p],
            send_sem=sems.at[g, d],
            recv_sem=sems.at[g, d],
            device_id=at_slot(p),
            device_id_type=MESH,
        ).wait_recv()

    def landed_all(buffer, sems, g):
        for d in range(1, 8):
            landed(buffer, sems, g, d)

        @pl.when(core == 1)
        def _():
            landed(buffer, sems, g, 0)

    def dispatch(g):
        held = {}

        def select():
            value = jnp.full((128, 128), -1.0, F32)
            for q in range(4):
                for c in range(2):
                    line = met[4 * g + q, pl.ds(2 * z + lax.rem(y + c, 2), 1), :]
                    value = jnp.where((row_q == q) & (row_c == c), line, value)
            rank_here = (
                jnp.where(value >= 2.0, 1.0, 0.0)
                + jnp.where(value >= 4.0, 1.0, 0.0)
                + jnp.where(value >= 6.0, 1.0, 0.0)
            )
            picked = (value >= 0.0) & (lane_g == row_x) & (rank_here == row_s.astype(F32))
            held["choose"] = folded(jnp.where(picked, 1.0, 0.0)).astype(BF)
            weigh = folded(jnp.where(picked, value - 2.0 * rank_here, 0.0))
            swt[g] = weigh.T.astype(BF)

        def pick(c):
            cols = slice(512 * c, 512 * c + 512)
            rows = tok[4 * g : 4 * g + 4, :, cols].reshape(128, 512)
            sent = jnp.dot(held["choose"], rows, preferred_element_type=F32).astype(BF)
            sendx[g, :, :, cols] = sent.reshape(8, 16, 512)

        def send():
            for d in range(1, 8):
                go(x_copy(g, d))

            @pl.when(core == 1)
            def _():
                x_copy(g, 0).start()

            @pl.when(core == 0)
            def _():
                rx[g, me8] = sendx[g, me8]

        return [select] + [functools.partial(pick, c) for c in range(4)] + [send]

    work = []

    def do_next():
        if work:
            work.pop(0)()

    def do_all():
        while work:
            do_next()

    for k in range(1, 9):
        for chunk in range(4):
            for dr in range(2):
                if chunk == 0 and (dr, k) in met_copy:
                    met_copy[dr, k].wait_recv()
                    if (dr, k + 1) in met_copy:
                        go(met_copy[dr, k + 1])
                if (dr, k, chunk) in tok_copy:
                    tok_copy[dr, k, chunk].wait_recv()
                    if (dr, k + 1, chunk) in tok_copy:
                        go(tok_copy[dr, k + 1, chunk])
            do_next()
        if k % 2 == 0:
            work.extend(dispatch(k // 2 - 1))
        if k == 2:
            work.append(functools.partial(send_weights, 2, 0))
            work.append(functools.partial(send_weights, 2, 1))
        if k == 6:
            work.append(functools.partial(pass_on, 1))
    do_all()

    for g in range(4):
        landed_all(rx, x_r, g)

    def hidden_units(slot):
        def body(h, carry):
            rows = rx[pl.ds(2 * h, 2)].reshape(256, D)
            gate_pre = lax.dot_general(rows, wb[slot, 0:192], NT, preferred_element_type=F32)
            up_pre = lax.dot_general(rows, wb[slot, 192:384], NT, preferred_element_type=F32)
            activated = gate_pre * (1.0 / (1.0 + jnp.exp(-gate_pre))) * up_pre
            act[slot, pl.ds(pl.multiple_of(256 * h, 256), 256), :] = activated.astype(BF)
            return carry

        lax.fori_loop(0, 2, body, 0)

    weight_ready(0)
    weight_ready(1)
    hidden_units(0)
    hidden_units(1)
    pass_on(2)
    hidden_units(2)
    hidden_units(3)
    weight_ready(2)

    def project(g):
        for c in range(4):
            cols = slice(512 * c, 512 * c + 512)
            total = jnp.dot(
                act[0, 128 * g : 128 * g + 128, :],
                wb[0, 384:576, cols],
                preferred_element_type=F32,
            )
            for slot in range(1, 4):
                total = total + jnp.dot(
                    act[slot, 128 * g : 128 * g + 128, :],
                    wb[slot, 384:576, cols],
                    preferred_element_type=F32,
                )
            ysend[g, :, :, cols] = total.astype(BF).reshape(8, 16, 512)
        for d in range(1, 8):
            go(y_copy(g, d))

        @pl.when(core == 1)
        def _():
            y_copy(g, 0).start()

        @pl.when(core == 0)
        def _():
            ry[g, me8] = ysend[g, me8]

    for g in (3, 2, 1, 0):
        project(g)

    def gather_back(g):
        def wait():
            landed_all(ry, y_r, g)

        def weigh(c):
            cols = slice(512 * c, 512 * c + 512)
            rows = ry[g, :, :, cols].reshape(128, 512)
            mixed = jnp.dot(swt[g], rows, preferred_element_type=F32)
            part[4 * g : 4 * g + 4, :, cols] = mixed.reshape(4, 32, 512)

        return [wait] + [functools.partial(weigh, c) for c in range(4)]

    rs_copy = {}
    for dr in range(2):
        for j in range(8):
            for chunk in range(4):
                if j == 0 and chunk // 2 != dr:
                    continue
                rows, cols = pl.ds(16 * (chunk // 2), 16), pl.ds(1024 * (chunk % 2), 1024)
                rs_copy[dr, j, chunk] = pltpu.make_async_remote_copy(
                    src_ref=rss.at[dr, j, rows, cols],
                    dst_ref=rsr.at[dr, j, rows, cols],
                    send_sem=rs_s.at[dr, j, chunk],
                    recv_sem=rs_r.at[dr, j, chunk],
                    device_id=z_next[dr],
                    device_id_type=MESH,
                )

    work.extend(gather_back(3))
    do_all()
    for j in range(8):
        if j in (2, 4, 6):
            do_all()
        if j in (1, 3, 5):
            work.extend([lambda: None] * 2 + gather_back(2 - j // 2))
        for chunk in range(4):
            rows = slice(16 * (chunk // 2), 16 * (chunk // 2) + 16)
            cols = slice(1024 * (chunk % 2), 1024 * (chunk % 2) + 1024)
            for dr in range(2):
                if (dr, j, chunk) not in rs_copy:
                    continue
                total = part[slot_of(1 - dr, 8 - j), rows, cols]
                if (dr, j - 1, chunk) in rs_copy:
                    rs_copy[dr, j - 1, chunk].wait_recv()
                    total = total + rsr[dr, j - 1, rows, cols].astype(F32)
                rss[dr, j, rows, cols] = total.astype(BF)
                go(rs_copy[dr, j, chunk])
            do_next()
    for chunk in range(4):
        rows = slice(16 * (chunk // 2), 16 * (chunk // 2) + 16)
        cols = slice(1024 * (chunk % 2), 1024 * (chunk % 2) + 1024)
        total = hid[rows, cols] + part[0, rows, cols]
        for dr in range(2):
            rs_copy[dr, 7, chunk].wait_recv()
            total = total + rsr[dr, 7, rows, cols].astype(F32)
        out[rows, cols] = total.astype(BF)

    for copy in pending:
        copy.wait_send()

    @pl.when(core == 1)
    def _():
        for g in range(4):
            x_copy(g, 0).wait_send()
            y_copy(g, 0).wait_send()

    @pl.when(keeper)
    def _():
        for a in range(3):
            for half in range(2):
                for piece in range(2):
                    give(2, a, half, piece).wait_send()
            share_weight(a).wait_send()

    @pl.when(jnp.logical_not(keeper))
    def _():
        for a in range(3):
            for half in range(2):
                for piece in range(2):
                    give(0, a, half, piece).wait_send()
                    give(1, a, half, piece).wait_send()


def layer(*operands):
    vmem = pl.BlockSpec(memory_space=pltpu.VMEM)
    anywhere = pl.BlockSpec(memory_space=pl.ANY)
    dma = pltpu.SemaphoreType.DMA
    return pl.pallas_call(
        layer_kernel,
        out_shape=jax.ShapeDtypeStruct((TOK, D), BF),
        in_specs=[vmem] * 3 + [anywhere] * 2 + [vmem, anywhere] + [vmem] * 3 + [anywhere] * 3,
        out_specs=vmem,
        scratch_shapes=[
            pltpu.VMEM((TOK, D), BF),
            pltpu.VMEM((TOK, 256), BF),
            pltpu.VMEM((TOK, 256), BF),
            pltpu.VMEM((4, TOK, 512), BF),
            pltpu.VMEM((4, 256, 128), BF),
            pltpu.VMEM((4, 256, 128), BF),
            pltpu.VMEM((4, TOK, 128), BF),
            pltpu.VMEM((4, TOK, 128), BF),
            pltpu.VMEM((4, TOK, 512), BF),
            pltpu.VMEM((512, D), BF),
            pltpu.VMEM((4, TOK, D), BF),
            pltpu.VMEM((3, TOK, D), BF),
            pltpu.VMEM((TOK, D), F32),
            pltpu.VMEM((16, 128), F32),
            pltpu.VMEM((4, ZN, 2, 16, 128), BF),
            pltpu.VMEM((2048, 128), F32),
            pltpu.VMEM((128, D), BF),
            pltpu.VMEM((16, TOK, D), BF),
            pltpu.VMEM((16, TOK, 128), F32),
            pltpu.VMEM((4, 128, 128), BF),
            pltpu.VMEM((4, 8, 16, D), BF),
            pltpu.VMEM((4, 8, 16, D), BF),
            pltpu.VMEM((4, 512, 192), BF),
            pltpu.VMEM((4, 8, 16, D), BF),
            pltpu.VMEM((4, 8, 16, D), BF),
            pltpu.VMEM((16, TOK, D), F32),
            pltpu.VMEM((2, 8, TOK, D), BF),
            pltpu.VMEM((2, 8, TOK, D), BF),
            pltpu.VMEM((4, 576, D), BF),
            dma((3, 5)), dma((3, 5)), dma((6,)),
            dma((3,)), dma((3,)),
            dma((15,)), dma((15,)),
            dma((7,)), dma((7,)),
            dma((2, 8, 4)), dma((2, 8, 4)),
            dma((2, 8)), dma((2, 8)),
            dma((4, 8)), dma((4, 8)),
            dma((4, 8)), dma((4, 8)),
            dma((2, 8, 4)), dma((2, 8, 4)),
            dma((3, 3, 2, 2)), dma((3, 3, 2)),
            dma((3, 3)), dma((3, 3)),
            dma((3,)), dma((3,)),
            dma((3,)),
        ],
        compiler_params=pltpu.CompilerParams(
            collective_id=0, has_side_effects=True, vmem_limit_bytes=56 * 1024 * 1024
        ),
        cost_estimate=pl.CostEstimate(
            flops=2 * 3 * 512 * 2048 * 768, bytes_accessed=8 << 20, transcendentals=512 * 768
        ),
    )(*operands)


def per_device(
    queries,
    block_keys,
    block_values,
    cache_keys,
    cache_values,
    residual,
    out_weight,
    norm_gain,
    router,
    gate_weight,
    up_weight,
    down_weight,
    expert_ids,
):
    block_output = layer(
        queries,
        block_keys,
        block_values,
        cache_keys.reshape(256, 256),
        cache_values.reshape(256, 256),
        residual,
        out_weight,
        norm_gain.reshape(1, D),
        router.T,
        expert_ids,
        gate_weight[0].T,
        up_weight[0].T,
        down_weight[0].T,
    )
    return block_output.reshape(residual.shape)


def solution(mesh):
    in_specs = (
        P("exp", "ctx", None, None),
        P("exp", "ctx", None, None),
        P("exp", "ctx", None, None),
        P("exp", "ctx", None),
        P("exp", "ctx", None),
        P("exp", "ctx", None, None),
        P("ctx", None),
        P(),
        P(None, "exp"),
        P("exp", None, "ctx"),
        P("exp", None, "ctx"),
        P("exp", None, "ctx"),
        P("exp", "ctx", None, None),
    )
    out_specs = P("exp", "ctx", None, None)
    return jax.shard_map(
        per_device, mesh=mesh, in_specs=in_specs, out_specs=out_specs, check_vma=False
    )
```

```python
import functools

import jax
import jax.numpy as jnp
from jax import lax
from jax.experimental import pallas as pl
from jax.experimental.pallas import tpu as pltpu
from jax.sharding import PartitionSpec as P

D = 2048
HEAD_DIM = 128
TOPK = 8


MESH = pl.DeviceIdType.MESH
BF = jnp.bfloat16
F32 = jnp.float32
NT = (((1,), (1,)), ((), ()))
TOK = 32
ZN = 16


def slot_of(direction, distance):
    if distance == 8:
        return 15
    return 2 * distance - 1 + direction


def layer_kernel(
    q_in, bk_in, bv_in, cache_keys, cache_values, residual, out_weight,
    gain, router, ids, gate, up, down, out,
    queries, block_keys, block_values, q_all, k_all, v_all, bk_all, bv_all, att, ow, psend, precv, hid, rt, rg, rgf, rfull,
    tok, met, swt, sendx, rx, act, ysend, ry, part, rss, rsr, wb,
    ex_s, ex_r, own_l, p_s, p_r, rz_s, rz_r, rp_s, rp_r,
    tok_s, tok_r, met_s, met_r, x_s, x_r, y_s, y_r, rs_s, rs_r,
    w_s, w_r, v_s, v_r, o_s, o_r, loc,
):
    y = lax.axis_index("ctx")
    e = lax.axis_index("exp")
    core = lax.rem(e, 2)
    z = lax.rem(e // 2, ZN)
    x = e // 32
    me8 = x * 2 + core

    def at_z(other):
        return (y, x * 32 + other * 2 + core)

    def at_peer(p):
        return (y, (p // 2) * 32 + z * 2 + lax.rem(p, 2))

    def at_slot(p):
        kept = lax.rem(p, 2)
        return (lax.rem(y + kept * (1 + 2 * core), 4), (p // 2) * 32 + z * 2 + kept)

    def at_source(p):
        other = lax.rem(p, 2)
        return (lax.rem(y + core * (3 - 2 * other), 4), (p // 2) * 32 + z * 2 + other)

    def at_line(d, c):
        return (lax.rem(y + d, 4), x * 32 + z * 2 + c)

    def at_y(d):
        return at_line(d, core)

    def at_across(d, k, c):
        return (lax.rem(y + d, 4), lax.rem(x + k, 4) * 32 + z * 2 + c)

    z_next = (at_z(lax.rem(z + 1, ZN)), at_z(lax.rem(z + ZN - 1, ZN)))
    sibling = at_line(0, 1 - core)
    keeper = core == lax.rem(y, 2)

    pending = []

    def go(copy):
        copy.start()
        pending.append(copy)
        return copy

    barrier = pltpu.get_barrier_semaphore()

    def greet(target):
        pl.semaphore_signal(barrier, inc=1, device_id=target, device_id_type=MESH)

    for d in range(1, ZN):
        greet(at_z(lax.rem(z + d, ZN)))
    for d in range(1, 8):
        greet(at_peer(lax.rem(me8 + d, 8)))
    for d in range(1, 4):
        for c in range(2):
            greet(at_line(d, c))

    @pl.when(core == 0)
    def _():
        for k in range(1, 4):
            greet(at_across(1, k, 1))

    @pl.when(core == 1)
    def _():
        for k in range(1, 4):
            greet(at_across(3, k, 0))
            greet(at_across(3, k, 1))
            greet(at_across(1, k, 1))

    weights = (gate, up, down)
    own_copies = []

    def own_weight(a):
        return pltpu.make_async_copy(weights[a], wb.at[0, pl.ds(192 * a, 192)], loc.at[a])

    @pl.when(keeper)
    def _():
        for a in range(3):
            own_weight(a).start()

    queries[...] = q_in[...].reshape(TOK, D)
    block_keys[...] = bk_in[...].reshape(TOK, 256)
    block_values[...] = bv_in[...].reshape(TOK, 256)
    for k in range(16):
        rt[k : k + 1, :] = router[0:1, 128 * k : 128 * k + 128].astype(F32)
    rg[x, z, core] = rt[...].astype(BF)

    def columns(index, width):
        return pl.ds(pl.multiple_of(index * width, width), width)

    def shares(owner):
        group = owner // 2
        return (
            queries.at[:, columns(owner, 512)],
            cache_keys.at[:, columns(group, 128)],
            cache_values.at[:, columns(group, 128)],
            block_keys.at[:, columns(group, 128)],
            block_values.at[:, columns(group, 128)],
        )

    gathered = (q_all, k_all, v_all, bk_all, bv_all)
    for a, share in enumerate(shares(y)):
        copy = pltpu.make_async_copy(share, gathered[a].at[y], own_l.at[a])
        copy.start()
        own_copies.append(copy)
    copy = pltpu.make_async_copy(out_weight, ow, own_l.at[5])
    copy.start()
    own_copies.append(copy)

    pl.semaphore_wait(barrier, 31 + 6 * core)

    def router_row(d, landed_here):
        held = lax.rem(z + ZN - d, ZN) if landed_here else z
        return pltpu.make_async_remote_copy(
            src_ref=rg.at[x, held, core],
            dst_ref=rg.at[x, held, core],
            send_sem=rz_s.at[d - 1],
            recv_sem=rz_r.at[d - 1],
            device_id=at_z(lax.rem(z + d, ZN)),
            device_id_type=MESH,
        )

    for d in range(1, ZN):
        go(router_row(d, False))

    def exchange(d, a):
        owner = lax.rem(y + d, 4)
        return pltpu.make_async_remote_copy(
            src_ref=shares(owner)[a],
            dst_ref=gathered[a].at[y],
            send_sem=ex_s.at[d - 1, a],
            recv_sem=ex_r.at[d - 1, a],
            device_id=at_y(d),
            device_id_type=MESH,
        )

    def exchanged(d, a):
        source = lax.rem(y + 4 - d, 4)
        pltpu.make_async_remote_copy(
            src_ref=gathered[a].at[source],
            dst_ref=gathered[a].at[source],
            send_sem=ex_s.at[d - 1, a],
            recv_sem=ex_r.at[d - 1, a],
            device_id=at_y(d),
            device_id_type=MESH,
        ).wait_recv()

    for d in (2, 1, 3):
        for a in range(5):
            go(exchange(d, a))

    def router_rows(d, landed_here):
        p = lax.rem(me8 + 8 - d, 8) if landed_here else me8
        return pltpu.make_async_remote_copy(
            src_ref=rg.at[p // 2, :, lax.rem(p, 2)],
            dst_ref=rg.at[p // 2, :, lax.rem(p, 2)],
            send_sem=rp_s.at[d - 1],
            recv_sem=rp_r.at[d - 1],
            device_id=at_peer(lax.rem(me8 + d, 8)),
            device_id_type=MESH,
        )

    pieces = ((0, 32), (32, 32), (64, 32))

    def give(dr, a, half, piece):
        start, count = pieces[piece]
        rows = pl.ds(192 * a + 96 * half + start, count)
        return pltpu.make_async_remote_copy(
            src_ref=weights[a].at[pl.ds(96 * half + start, count)],
            dst_ref=wb.at[1 + dr, rows],
            send_sem=w_s.at[dr, a, half, piece],
            recv_sem=w_r.at[dr, a, piece],
            device_id=at_line((1, 3, 2)[dr], half),
            device_id_type=MESH,
        )

    def share_weight(a):
        return pltpu.make_async_remote_copy(
            src_ref=weights[a],
            dst_ref=wb.at[0, pl.ds(192 * a, 192)],
            send_sem=o_s.at[a],
            recv_sem=o_r.at[a],
            device_id=sibling,
            device_id_type=MESH,
        )

    def send_weights(a, piece):
        @pl.when(keeper)
        def _():
            for half in range(2):
                give(2, a, half, piece).start()
            if piece == 0:
                share_weight(a).start()

        @pl.when(jnp.logical_not(keeper))
        def _():
            for half in range(2):
                give(0, a, half, piece).start()
                give(1, a, half, piece).start()

    def given(slot, a, piece):
        start, count = pieces[piece]
        rows = pl.ds(pl.multiple_of(192 * a + 96 * core + start, 32), count)
        pltpu.make_async_remote_copy(
            src_ref=wb.at[slot, rows],
            dst_ref=wb.at[slot, rows],
            send_sem=v_s.at[slot - 1, a, piece],
            recv_sem=w_r.at[slot - 1, a, piece],
            device_id=sibling,
            device_id_type=MESH,
        ).wait_recv()

    def half_copy(slot, a, half, start, count):
        rows = pl.ds(pl.multiple_of(192 * a + 96 * half + start, 32), count)
        return pltpu.make_async_remote_copy(
            src_ref=wb.at[slot, rows],
            dst_ref=wb.at[slot, rows],
            send_sem=v_s.at[slot - 1, a, start // 32],
            recv_sem=v_r.at[slot - 1, a, start // 32],
            device_id=sibling,
            device_id_type=MESH,
        )

    def pass_on(a):
        for slot in range(1, 4):
            for piece in range(3):
                given(slot, a, piece)
            go(half_copy(slot, a, core, 0, 96))

    def pass_piece(a, piece):
        for slot in range(1, 4):
            given(slot, a, piece)
            go(half_copy(slot, a, core, *pieces[piece]))

    def weight_ready(a):
        for slot in range(1, 4):
            for start, count in pieces if a == 2 else ((0, 96),):
                half_copy(slot, a, 1 - core, start, count).wait_recv()

        @pl.when(keeper)
        def _():
            own_weight(a).wait()

        @pl.when(jnp.logical_not(keeper))
        def _():
            share_weight(a).wait_recv()

    send_weights(0, 0)
    for d in range(1, ZN):
        router_row(d, True).wait_recv()
    for d in range(1, 8):
        go(router_rows(d, False))

    for copy in own_copies:
        copy.wait()
    for d in range(1, 4):
        for a in range(5):
            exchanged(d, a)

    key_step = lax.rem(lax.broadcasted_iota(jnp.int32, (256, 64), 1), 2)
    row_step = lax.rem(lax.broadcasted_iota(jnp.int32, (256, 64), 0), 2)
    for r in range(2):
        near, far = slice(16 * r, 16 * r + 16), slice(128 * r, 128 * r + 128)
        q_rows = jnp.concatenate(
            [q_all[m, near, 128 * h : 128 * h + 128] for h in range(4) for m in range(4)], 0
        )
        far_scores = lax.dot_general(
            q_rows, k_all[:, far, :].reshape(512, 128), NT, preferred_element_type=F32
        )
        near_scores = lax.dot_general(
            q_rows, bk_all[:, near, :].reshape(64, 128), NT, preferred_element_type=F32
        )
        far_scores = far_scores * HEAD_DIM ** (-0.5)
        near_scores = jnp.where(
            key_step == row_step, near_scores * HEAD_DIM ** (-0.5), -3e38
        )
        row_top = jnp.maximum(
            jnp.max(far_scores, -1, keepdims=True), jnp.max(near_scores, -1, keepdims=True)
        )
        far_exp = jnp.exp(far_scores - row_top)
        near_exp = jnp.where(key_step == row_step, jnp.exp(near_scores - row_top), 0.0)
        total = jnp.sum(far_exp, -1, keepdims=True) + jnp.sum(near_exp, -1, keepdims=True)
        weighted = jnp.dot(
            far_exp.astype(BF), v_all[:, far, :].reshape(512, 128), preferred_element_type=F32
        ) + jnp.dot(
            near_exp.astype(BF), bv_all[:, near, :].reshape(64, 128), preferred_element_type=F32
        )
        attended = (weighted / total).astype(BF)
        for h in range(4):
            for m in range(4):
                att[m, near, 128 * h : 128 * h + 128] = attended[
                    64 * h + 16 * m : 64 * h + 16 * m + 16
                ]

    for c in range(4):
        cols = slice(512 * c, 512 * c + 512)
        projected = jnp.dot(
            att[...].reshape(128, 512), ow[:, cols], preferred_element_type=F32
        ).reshape(4, TOK, 512)
        part[0:4, :, cols] = projected
        psend[:, :, cols] = projected.astype(BF)

    p_copy = []
    for d in (2, 1, 3):
        p_copy.append(
            pltpu.make_async_remote_copy(
                src_ref=psend.at[lax.rem(y + d, 4)],
                dst_ref=precv.at[d - 1],
                send_sem=p_s.at[d - 1],
                recv_sem=p_r.at[d - 1],
                device_id=at_y(d),
                device_id_type=MESH,
            )
        )
        go(p_copy[-1])
    for a, piece in ((0, 1), (0, 2), (1, 0), (1, 1), (1, 2)):
        send_weights(a, piece)

    for d in range(1, 8):
        router_rows(d, True).wait_recv()
    rgf[...] = rg[...].reshape(2048, 128).astype(F32)
    for k in range(16):
        rfull[:, 128 * k : 128 * k + 128] = rgf[pl.ds(k, 128, stride=16), :].astype(BF)

    for copy in p_copy:
        copy.wait_recv()
    hidden = residual[...].reshape(TOK, D).astype(F32) + part[y]
    for d in range(3):
        hidden = hidden + precv[d].astype(F32)
    hid[...] = hidden
    scale = lax.rsqrt(jnp.mean(hidden * hidden, -1, keepdims=True) + 1e-06)
    normed = (hidden * scale * gain[...]).astype(BF)
    tok[0] = normed
    scores = lax.dot_general(rfull[...], normed, NT, preferred_element_type=F32)
    scores = scores.astype(BF).astype(F32)
    id_rows = ids[...].reshape(TOK, TOPK)
    expert_lane = lax.broadcasted_iota(jnp.int32, (TOK, 128), 1)
    named = expert_lane == id_rows[:, 0:1]
    for k in range(1, TOPK):
        named = named | (expert_lane == id_rows[:, k : k + 1])
    hits = jnp.where(named, 1.0, 0.0).T
    named = hits > 0.0
    top = jnp.max(jnp.where(named, scores, -3e38), 0, keepdims=True)
    grown = jnp.where(named, jnp.exp(jnp.minimum(scores - top, 0.0)), 0.0)
    mix = grown / jnp.sum(grown, 0, keepdims=True)
    before = lax.broadcasted_iota(jnp.int32, (TOK, TOK), 0) < lax.broadcasted_iota(
        jnp.int32, (TOK, TOK), 1
    )
    rank = jnp.dot(
        hits.astype(BF), jnp.where(before, 1.0, 0.0).astype(BF), preferred_element_type=F32
    )
    code = jnp.where(named, 2.0 * rank + mix, -1.0)
    for k in range(4):
        met[0, :, 32 * k : 32 * k + 32] = code[32 * k : 32 * k + 32, :]

    tok_copy, met_copy = {}, {}
    for dr in range(2):
        for k in range(1, 9):
            src = 0 if k == 1 else slot_of(dr, k - 1)
            dst = slot_of(dr, k)
            for chunk in range(4):
                if k == 8 and chunk // 2 != dr:
                    continue
                rows, cols = pl.ds(16 * (chunk // 2), 16), pl.ds(1024 * (chunk % 2), 1024)
                tok_copy[dr, k, chunk] = pltpu.make_async_remote_copy(
                    src_ref=tok.at[src, rows, cols],
                    dst_ref=tok.at[dst, rows, cols],
                    send_sem=tok_s.at[dr, k - 1, chunk],
                    recv_sem=tok_r.at[dr, k - 1, chunk],
                    device_id=z_next[dr],
                    device_id_type=MESH,
                )
            if k < 8 or dr == 0:
                met_copy[dr, k] = pltpu.make_async_remote_copy(
                    src_ref=met.at[src],
                    dst_ref=met.at[dst],
                    send_sem=met_s.at[dr, k - 1],
                    recv_sem=met_r.at[dr, k - 1],
                    device_id=z_next[dr],
                    device_id_type=MESH,
                )

    for dr in range(2):
        go(met_copy[dr, 1])
    for chunk in range(4):
        for dr in range(2):
            go(tok_copy[dr, 1, chunk])
    pass_on(0)

    row = lax.broadcasted_iota(jnp.int32, (128, 128), 0)
    lane = lax.broadcasted_iota(jnp.int32, (128, 128), 1)
    row_x, row_c = row // 32, lax.rem(row // 16, 2)
    row_q, row_s = lax.rem(row // 4, 4), lax.rem(row, 4)
    lane_g = lane // 32

    def folded(values):
        total = values
        for k in range(1, 4):
            total = total + pltpu.roll(values, 32 * k, 1)
        return jnp.where(lane_g == row_q, total, 0.0)

    def x_copy(g, d):
        p = lax.rem(me8 + d, 8)
        return pltpu.make_async_remote_copy(
            src_ref=sendx.at[g, p],
            dst_ref=rx.at[g, me8],
            send_sem=x_s.at[g, d],
            recv_sem=x_r.at[g, d],
            device_id=at_slot(p),
            device_id_type=MESH,
        )

    def y_copy(g, d):
        p = lax.rem(me8 + d, 8)
        return pltpu.make_async_remote_copy(
            src_ref=ysend.at[g, p],
            dst_ref=ry.at[g, me8],
            send_sem=y_s.at[g, d],
            recv_sem=y_r.at[g, d],
            device_id=at_source(p),
            device_id_type=MESH,
        )

    def landed(buffer, sems, g, d):
        p = lax.rem(me8 + 8 - d, 8)
        pltpu.make_async_remote_copy(
            src_ref=buffer.at[g, p],
            dst_ref=buffer.at[g, p],
            send_sem=sems.at[g, d],
            recv_sem=sems.at[g, d],
            device_id=at_slot(p),
            device_id_type=MESH,
        ).wait_recv()

    def landed_all(buffer, sems, g):
        for d in range(1, 8):
            landed(buffer, sems, g, d)

        @pl.when(core == 1)
        def _():
            landed(buffer, sems, g, 0)

    def dispatch(g):
        held = {}

        def select():
            value = jnp.full((128, 128), -1.0, F32)
            for q in range(4):
                for c in range(2):
                    line = met[4 * g + q, pl.ds(2 * z + lax.rem(y + c, 2), 1), :]
                    value = jnp.where((row_q == q) & (row_c == c), line, value)
            rank_here = (
                jnp.where(value >= 2.0, 1.0, 0.0)
                + jnp.where(value >= 4.0, 1.0, 0.0)
                + jnp.where(value >= 6.0, 1.0, 0.0)
            )
            picked = (value >= 0.0) & (lane_g == row_x) & (rank_here == row_s.astype(F32))
            held["choose"] = folded(jnp.where(picked, 1.0, 0.0)).astype(BF)
            weigh = folded(jnp.where(picked, value - 2.0 * rank_here, 0.0))
            swt[g] = weigh.T.astype(BF)

        def pick(c):
            cols = slice(512 * c, 512 * c + 512)
            rows = tok[4 * g : 4 * g + 4, :, cols].reshape(128, 512)
            sent = jnp.dot(held["choose"], rows, preferred_element_type=F32).astype(BF)
            sendx[g, :, :, cols] = sent.reshape(8, 16, 512)

        def send():
            for d in range(1, 8):
                go(x_copy(g, d))

            @pl.when(core == 1)
            def _():
                x_copy(g, 0).start()

            @pl.when(core == 0)
            def _():
                rx[g, me8] = sendx[g, me8]

        return [select] + [functools.partial(pick, c) for c in range(4)] + [send]

    work = []

    def do_next():
        if work:
            work.pop(0)()

    def do_all():
        while work:
            do_next()

    for k in range(1, 9):
        for chunk in range(4):
            for dr in range(2):
                if chunk == 0 and (dr, k) in met_copy:
                    met_copy[dr, k].wait_recv()
                    if (dr, k + 1) in met_copy:
                        go(met_copy[dr, k + 1])
                if (dr, k, chunk) in tok_copy:
                    tok_copy[dr, k, chunk].wait_recv()
                    if (dr, k + 1, chunk) in tok_copy:
                        go(tok_copy[dr, k + 1, chunk])
            do_next()
        if k % 2 == 0:
            work.extend(dispatch(k // 2 - 1))
        if k == 2:
            work.append(functools.partial(send_weights, 2, 0))
        if k == 5:
            work.append(functools.partial(send_weights, 2, 1))
        if k == 6:
            work.append(functools.partial(pass_on, 1))
    do_all()

    send_weights(2, 2)

    def hidden_units(slot, h):
        rows = rx[2 * h : 2 * h + 2].reshape(256, D)
        gate_pre = lax.dot_general(rows, wb[slot, 0:192], NT, preferred_element_type=F32)
        up_pre = lax.dot_general(rows, wb[slot, 192:384], NT, preferred_element_type=F32)
        activated = gate_pre * (1.0 / (1.0 + jnp.exp(-gate_pre))) * up_pre
        act[slot, 256 * h : 256 * h + 256, :] = activated.astype(BF)

    landed_all(rx, x_r, 0)
    landed_all(rx, x_r, 1)
    weight_ready(0)
    weight_ready(1)
    for slot in range(4):
        hidden_units(slot, 0)
    pass_piece(2, 0)
    pass_piece(2, 1)
    landed_all(rx, x_r, 2)
    landed_all(rx, x_r, 3)
    for slot in range(4):
        hidden_units(slot, 1)
    pass_piece(2, 2)
    weight_ready(2)

    def project(g):
        for c in range(4):
            cols = slice(512 * c, 512 * c + 512)
            total = jnp.dot(
                act[0, 128 * g : 128 * g + 128, :],
                wb[0, 384:576, cols],
                preferred_element_type=F32,
            )
            for slot in range(1, 4):
                total = total + jnp.dot(
                    act[slot, 128 * g : 128 * g + 128, :],
                    wb[slot, 384:576, cols],
                    preferred_element_type=F32,
                )
            ysend[g, :, :, cols] = total.astype(BF).reshape(8, 16, 512)
        for d in range(1, 8):
            go(y_copy(g, d))

        @pl.when(core == 1)
        def _():
            y_copy(g, 0).start()

        @pl.when(core == 0)
        def _():
            ry[g, me8] = ysend[g, me8]

    for g in (3, 2, 1, 0):
        project(g)

    def gather_back(g):
        def wait():
            landed_all(ry, y_r, g)

        def weigh(c):
            cols = slice(512 * c, 512 * c + 512)
            rows = ry[g, :, :, cols].reshape(128, 512)
            mixed = jnp.dot(swt[g], rows, preferred_element_type=F32)
            part[4 * g : 4 * g + 4, :, cols] = mixed.reshape(4, 32, 512)

        return [wait] + [functools.partial(weigh, c) for c in range(4)]

    rs_copy = {}
    for dr in range(2):
        for j in range(8):
            for chunk in range(4):
                if j == 0 and chunk // 2 != dr:
                    continue
                rows, cols = pl.ds(16 * (chunk // 2), 16), pl.ds(1024 * (chunk % 2), 1024)
                rs_copy[dr, j, chunk] = pltpu.make_async_remote_copy(
                    src_ref=rss.at[dr, j, rows, cols],
                    dst_ref=rsr.at[dr, j, rows, cols],
                    send_sem=rs_s.at[dr, j, chunk],
                    recv_sem=rs_r.at[dr, j, chunk],
                    device_id=z_next[dr],
                    device_id_type=MESH,
                )

    work.extend(gather_back(3))
    do_all()
    for j in range(8):
        if j in (2, 4, 6):
            do_all()
        if j in (1, 3, 5):
            work.extend([lambda: None] * 2 + gather_back(2 - j // 2))
        for chunk in range(4):
            rows = slice(16 * (chunk // 2), 16 * (chunk // 2) + 16)
            cols = slice(1024 * (chunk % 2), 1024 * (chunk % 2) + 1024)
            for dr in range(2):
                if (dr, j, chunk) not in rs_copy:
                    continue
                total = part[slot_of(1 - dr, 8 - j), rows, cols]
                if (dr, j - 1, chunk) in rs_copy:
                    rs_copy[dr, j - 1, chunk].wait_recv()
                    total = total + rsr[dr, j - 1, rows, cols].astype(F32)
                rss[dr, j, rows, cols] = total.astype(BF)
                go(rs_copy[dr, j, chunk])
            do_next()
    for chunk in range(4):
        rows = slice(16 * (chunk // 2), 16 * (chunk // 2) + 16)
        cols = slice(1024 * (chunk % 2), 1024 * (chunk % 2) + 1024)
        total = hid[rows, cols] + part[0, rows, cols]
        for dr in range(2):
            rs_copy[dr, 7, chunk].wait_recv()
            total = total + rsr[dr, 7, rows, cols].astype(F32)
        out[rows, cols] = total.astype(BF)

    for copy in pending:
        copy.wait_send()

    @pl.when(core == 1)
    def _():
        for g in range(4):
            x_copy(g, 0).wait_send()
            y_copy(g, 0).wait_send()

    @pl.when(keeper)
    def _():
        for a in range(3):
            for half in range(2):
                for piece in range(3):
                    give(2, a, half, piece).wait_send()
            share_weight(a).wait_send()

    @pl.when(jnp.logical_not(keeper))
    def _():
        for a in range(3):
            for half in range(2):
                for piece in range(3):
                    give(0, a, half, piece).wait_send()
                    give(1, a, half, piece).wait_send()


def layer(*operands):
    vmem = pl.BlockSpec(memory_space=pltpu.VMEM)
    anywhere = pl.BlockSpec(memory_space=pl.ANY)
    dma = pltpu.SemaphoreType.DMA
    return pl.pallas_call(
        layer_kernel,
        out_shape=jax.ShapeDtypeStruct((TOK, D), BF),
        in_specs=[vmem] * 3 + [anywhere] * 2 + [vmem, anywhere] + [vmem] * 3 + [anywhere] * 3,
        out_specs=vmem,
        scratch_shapes=[
            pltpu.VMEM((TOK, D), BF),
            pltpu.VMEM((TOK, 256), BF),
            pltpu.VMEM((TOK, 256), BF),
            pltpu.VMEM((4, TOK, 512), BF),
            pltpu.VMEM((4, 256, 128), BF),
            pltpu.VMEM((4, 256, 128), BF),
            pltpu.VMEM((4, TOK, 128), BF),
            pltpu.VMEM((4, TOK, 128), BF),
            pltpu.VMEM((4, TOK, 512), BF),
            pltpu.VMEM((512, D), BF),
            pltpu.VMEM((4, TOK, D), BF),
            pltpu.VMEM((3, TOK, D), BF),
            pltpu.VMEM((TOK, D), F32),
            pltpu.VMEM((16, 128), F32),
            pltpu.VMEM((4, ZN, 2, 16, 128), BF),
            pltpu.VMEM((2048, 128), F32),
            pltpu.VMEM((128, D), BF),
            pltpu.VMEM((16, TOK, D), BF),
            pltpu.VMEM((16, TOK, 128), F32),
            pltpu.VMEM((4, 128, 128), BF),
            pltpu.VMEM((4, 8, 16, D), BF),
            pltpu.VMEM((4, 8, 16, D), BF),
            pltpu.VMEM((4, 512, 192), BF),
            pltpu.VMEM((4, 8, 16, D), BF),
            pltpu.VMEM((4, 8, 16, D), BF),
            pltpu.VMEM((16, TOK, D), F32),
            pltpu.VMEM((2, 8, TOK, D), BF),
            pltpu.VMEM((2, 8, TOK, D), BF),
            pltpu.VMEM((4, 576, D), BF),
            dma((3, 5)), dma((3, 5)), dma((6,)),
            dma((3,)), dma((3,)),
            dma((15,)), dma((15,)),
            dma((7,)), dma((7,)),
            dma((2, 8, 4)), dma((2, 8, 4)),
            dma((2, 8)), dma((2, 8)),
            dma((4, 8)), dma((4, 8)),
            dma((4, 8)), dma((4, 8)),
            dma((2, 8, 4)), dma((2, 8, 4)),
            dma((3, 3, 2, 3)), dma((3, 3, 3)),
            dma((3, 3, 3)), dma((3, 3, 3)),
            dma((3,)), dma((3,)),
            dma((3,)),
        ],
        compiler_params=pltpu.CompilerParams(
            collective_id=0, has_side_effects=True, vmem_limit_bytes=56 * 1024 * 1024
        ),
        cost_estimate=pl.CostEstimate(
            flops=2 * 3 * 512 * 2048 * 768, bytes_accessed=8 << 20, transcendentals=512 * 768
        ),
    )(*operands)


def per_device(
    queries,
    block_keys,
    block_values,
    cache_keys,
    cache_values,
    residual,
    out_weight,
    norm_gain,
    router,
    gate_weight,
    up_weight,
    down_weight,
    expert_ids,
):
    block_output = layer(
        queries,
        block_keys,
        block_values,
        cache_keys.reshape(256, 256),
        cache_values.reshape(256, 256),
        residual,
        out_weight,
        norm_gain.reshape(1, D),
        router.T,
        expert_ids,
        gate_weight[0].T,
        up_weight[0].T,
        down_weight[0].T,
    )
    return block_output.reshape(residual.shape)


def solution(mesh):
    in_specs = (
        P("exp", "ctx", None, None),
        P("exp", "ctx", None, None),
        P("exp", "ctx", None, None),
        P("exp", "ctx", None),
        P("exp", "ctx", None),
        P("exp", "ctx", None, None),
        P("ctx", None),
        P(),
        P(None, "exp"),
        P("exp", None, "ctx"),
        P("exp", None, "ctx"),
        P("exp", None, "ctx"),
        P("exp", "ctx", None, None),
    )
    out_specs = P("exp", "ctx", None, None)
    return jax.shard_map(
        per_device, mesh=mesh, in_specs=in_specs, out_specs=out_specs, check_vma=False
    )
```

```python
import functools

import jax
import jax.numpy as jnp
from jax import lax
from jax.experimental import pallas as pl
from jax.experimental.pallas import tpu as pltpu
from jax.sharding import PartitionSpec as P

D = 2048
HEAD_DIM = 128
TOPK = 8


MESH = pl.DeviceIdType.MESH
BF = jnp.bfloat16
F32 = jnp.float32
NT = (((1,), (1,)), ((), ()))
TOK = 32
ZN = 16


def slot_of(direction, distance):
    if distance == 8:
        return 15
    return 2 * distance - 1 + direction


def layer_kernel(
    q_in, bk_in, bv_in, cache_keys, cache_values, res_in, out_weight,
    gain, router, ids, gate, up, down, out,
    residual, queries, block_keys, block_values, q_all, k_all, v_all, bk_all, bv_all, att, ow, psend, precv, hid, rt, rg, rgf, rfull,
    tok, met, swt, sendx, rx, act, ysend, ry, part, rss, rsr, wb,
    ex_s, ex_r, own_l, p_s, p_r, rz_s, rz_r, rp_s, rp_r,
    tok_s, tok_r, met_s, met_r, x_s, x_r, y_s, y_r, rs_s, rs_r,
    w_s, w_r, v_s, v_r, o_s, o_r, loc,
):
    y = lax.axis_index("ctx")
    e = lax.axis_index("exp")
    core = lax.rem(e, 2)
    z = lax.rem(e // 2, ZN)
    x = e // 32
    me8 = x * 2 + core

    def at_z(other):
        return (y, x * 32 + other * 2 + core)

    def at_peer(p):
        return (y, (p // 2) * 32 + z * 2 + lax.rem(p, 2))

    def at_slot(p):
        kept = lax.rem(p, 2)
        return (lax.rem(y + kept * (1 + 2 * core), 4), (p // 2) * 32 + z * 2 + kept)

    def at_source(p):
        other = lax.rem(p, 2)
        return (lax.rem(y + core * (3 - 2 * other), 4), (p // 2) * 32 + z * 2 + other)

    def at_line(d, c):
        return (lax.rem(y + d, 4), x * 32 + z * 2 + c)

    def at_y(d):
        return at_line(d, core)

    def at_across(d, k, c):
        return (lax.rem(y + d, 4), lax.rem(x + k, 4) * 32 + z * 2 + c)

    z_next = (at_z(lax.rem(z + 1, ZN)), at_z(lax.rem(z + ZN - 1, ZN)))
    sibling = at_line(0, 1 - core)
    keeper = core == lax.rem(y, 2)

    pending = []

    def go(copy):
        copy.start()
        pending.append(copy)
        return copy

    barrier = pltpu.get_barrier_semaphore()

    def greet(target):
        pl.semaphore_signal(barrier, inc=1, device_id=target, device_id_type=MESH)

    for d in range(1, ZN):
        greet(at_z(lax.rem(z + d, ZN)))
    for d in range(1, 8):
        greet(at_peer(lax.rem(me8 + d, 8)))
    for d in range(1, 4):
        for c in range(2):
            greet(at_line(d, c))

    @pl.when(core == 0)
    def _():
        for k in range(1, 4):
            greet(at_across(1, k, 1))

    @pl.when(core == 1)
    def _():
        for k in range(1, 4):
            greet(at_across(3, k, 0))
            greet(at_across(3, k, 1))
            greet(at_across(1, k, 1))

    weights = (gate, up, down)
    own_copies = []

    def own_weight(a):
        return pltpu.make_async_copy(weights[a], wb.at[0, pl.ds(192 * a, 192)], loc.at[a])

    @pl.when(keeper)
    def _():
        for a in range(3):
            own_weight(a).start()

    queries[...] = q_in[...].reshape(TOK, D)
    block_keys[...] = bk_in[...].reshape(TOK, 256)
    block_values[...] = bv_in[...].reshape(TOK, 256)
    for k in range(16):
        rt[k : k + 1, :] = router[0:1, 128 * k : 128 * k + 128].astype(F32)
    rg[x, z, core] = rt[...].astype(BF)

    def columns(index, width):
        return pl.ds(pl.multiple_of(index * width, width), width)

    def shares(owner):
        group = owner // 2
        return (
            queries.at[:, columns(owner, 512)],
            cache_keys.at[:, columns(group, 128)],
            cache_values.at[:, columns(group, 128)],
            block_keys.at[:, columns(group, 128)],
            block_values.at[:, columns(group, 128)],
        )

    gathered = (q_all, k_all, v_all, bk_all, bv_all)
    for a, share in enumerate(shares(y)):
        copy = pltpu.make_async_copy(share, gathered[a].at[y], own_l.at[a])
        copy.start()
        own_copies.append(copy)
    copy = pltpu.make_async_copy(res_in, residual, own_l.at[6])
    copy.start()
    own_copies.append(copy)
    copy = pltpu.make_async_copy(out_weight, ow, own_l.at[5])
    copy.start()
    own_copies.append(copy)

    pl.semaphore_wait(barrier, 31 + 6 * core)

    def router_row(d, landed_here):
        held = lax.rem(z + ZN - d, ZN) if landed_here else z
        return pltpu.make_async_remote_copy(
            src_ref=rg.at[x, held, core],
            dst_ref=rg.at[x, held, core],
            send_sem=rz_s.at[d - 1],
            recv_sem=rz_r.at[d - 1],
            device_id=at_z(lax.rem(z + d, ZN)),
            device_id_type=MESH,
        )

    for d in range(1, ZN):
        go(router_row(d, False))

    def exchange(d, a):
        owner = lax.rem(y + d, 4)
        return pltpu.make_async_remote_copy(
            src_ref=shares(owner)[a],
            dst_ref=gathered[a].at[y],
            send_sem=ex_s.at[d - 1, a],
            recv_sem=ex_r.at[d - 1, a],
            device_id=at_y(d),
            device_id_type=MESH,
        )

    def exchanged(d, a):
        source = lax.rem(y + 4 - d, 4)
        pltpu.make_async_remote_copy(
            src_ref=gathered[a].at[source],
            dst_ref=gathered[a].at[source],
            send_sem=ex_s.at[d - 1, a],
            recv_sem=ex_r.at[d - 1, a],
            device_id=at_y(d),
            device_id_type=MESH,
        ).wait_recv()

    for d in (2, 1, 3):
        for a in range(5):
            go(exchange(d, a))

    def router_rows(d, landed_here):
        p = lax.rem(me8 + 8 - d, 8) if landed_here else me8
        return pltpu.make_async_remote_copy(
            src_ref=rg.at[p // 2, :, lax.rem(p, 2)],
            dst_ref=rg.at[p // 2, :, lax.rem(p, 2)],
            send_sem=rp_s.at[d - 1],
            recv_sem=rp_r.at[d - 1],
            device_id=at_peer(lax.rem(me8 + d, 8)),
            device_id_type=MESH,
        )

    pieces = ((0, 32), (32, 32), (64, 32))

    def give(dr, a, half, piece):
        start, count = pieces[piece]
        rows = pl.ds(192 * a + 96 * half + start, count)
        return pltpu.make_async_remote_copy(
            src_ref=weights[a].at[pl.ds(96 * half + start, count)],
            dst_ref=wb.at[1 + dr, rows],
            send_sem=w_s.at[dr, a, half, piece],
            recv_sem=w_r.at[dr, a, piece],
            device_id=at_line((1, 3, 2)[dr], half),
            device_id_type=MESH,
        )

    def share_weight(a):
        return pltpu.make_async_remote_copy(
            src_ref=weights[a],
            dst_ref=wb.at[0, pl.ds(192 * a, 192)],
            send_sem=o_s.at[a],
            recv_sem=o_r.at[a],
            device_id=sibling,
            device_id_type=MESH,
        )

    def send_weights(a, piece):
        @pl.when(keeper)
        def _():
            for half in range(2):
                give(2, a, half, piece).start()
            if piece == 0:
                share_weight(a).start()

        @pl.when(jnp.logical_not(keeper))
        def _():
            for half in range(2):
                give(0, a, half, piece).start()
                give(1, a, half, piece).start()

    def given(slot, a, piece):
        start, count = pieces[piece]
        rows = pl.ds(pl.multiple_of(192 * a + 96 * core + start, 32), count)
        pltpu.make_async_remote_copy(
            src_ref=wb.at[slot, rows],
            dst_ref=wb.at[slot, rows],
            send_sem=v_s.at[slot - 1, a, piece],
            recv_sem=w_r.at[slot - 1, a, piece],
            device_id=sibling,
            device_id_type=MESH,
        ).wait_recv()

    def half_copy(slot, a, half, start, count):
        rows = pl.ds(pl.multiple_of(192 * a + 96 * half + start, 32), count)
        return pltpu.make_async_remote_copy(
            src_ref=wb.at[slot, rows],
            dst_ref=wb.at[slot, rows],
            send_sem=v_s.at[slot - 1, a, start // 32],
            recv_sem=v_r.at[slot - 1, a, start // 32],
            device_id=sibling,
            device_id_type=MESH,
        )

    def pass_on(a):
        for slot in range(1, 4):
            for piece in range(3):
                given(slot, a, piece)
            go(half_copy(slot, a, core, 0, 96))

    def pass_piece(a, piece):
        for slot in range(1, 4):
            given(slot, a, piece)
            go(half_copy(slot, a, core, *pieces[piece]))

    def weight_ready(a):
        for slot in range(1, 4):
            for start, count in pieces if a == 2 else ((0, 96),):
                half_copy(slot, a, 1 - core, start, count).wait_recv()

        @pl.when(keeper)
        def _():
            own_weight(a).wait()

        @pl.when(jnp.logical_not(keeper))
        def _():
            share_weight(a).wait_recv()

    send_weights(0, 0)
    send_weights(0, 1)
    for d in range(1, ZN):
        router_row(d, True).wait_recv()
    for d in range(1, 8):
        go(router_rows(d, False))

    for copy in own_copies:
        copy.wait()
    for d in range(1, 4):
        for a in range(5):
            exchanged(d, a)

    key_step = lax.rem(lax.broadcasted_iota(jnp.int32, (256, 64), 1), 2)
    row_step = lax.rem(lax.broadcasted_iota(jnp.int32, (256, 64), 0), 2)
    for r in range(2):
        near, far = slice(16 * r, 16 * r + 16), slice(128 * r, 128 * r + 128)
        q_rows = jnp.concatenate(
            [q_all[m, near, 128 * h : 128 * h + 128] for h in range(4) for m in range(4)], 0
        )
        far_scores = lax.dot_general(
            q_rows, k_all[:, far, :].reshape(512, 128), NT, preferred_element_type=F32
        )
        near_scores = lax.dot_general(
            q_rows, bk_all[:, near, :].reshape(64, 128), NT, preferred_element_type=F32
        )
        far_scores = far_scores * HEAD_DIM ** (-0.5)
        near_scores = jnp.where(
            key_step == row_step, near_scores * HEAD_DIM ** (-0.5), -3e38
        )
        row_top = jnp.maximum(
            jnp.max(far_scores, -1, keepdims=True), jnp.max(near_scores, -1, keepdims=True)
        )
        far_exp = jnp.exp(far_scores - row_top)
        near_exp = jnp.where(key_step == row_step, jnp.exp(near_scores - row_top), 0.0)
        total = jnp.sum(far_exp, -1, keepdims=True) + jnp.sum(near_exp, -1, keepdims=True)
        weighted = jnp.dot(
            far_exp.astype(BF), v_all[:, far, :].reshape(512, 128), preferred_element_type=F32
        ) + jnp.dot(
            near_exp.astype(BF), bv_all[:, near, :].reshape(64, 128), preferred_element_type=F32
        )
        attended = (weighted / total).astype(BF)
        for h in range(4):
            for m in range(4):
                att[m, near, 128 * h : 128 * h + 128] = attended[
                    64 * h + 16 * m : 64 * h + 16 * m + 16
                ]

    for c in range(4):
        cols = slice(512 * c, 512 * c + 512)
        projected = jnp.dot(
            att[...].reshape(128, 512), ow[:, cols], preferred_element_type=F32
        ).reshape(4, TOK, 512)
        part[0:4, :, cols] = projected
        psend[:, :, cols] = projected.astype(BF)

    p_copy = []
    for d in (2, 1, 3):
        p_copy.append(
            pltpu.make_async_remote_copy(
                src_ref=psend.at[lax.rem(y + d, 4)],
                dst_ref=precv.at[d - 1],
                send_sem=p_s.at[d - 1],
                recv_sem=p_r.at[d - 1],
                device_id=at_y(d),
                device_id_type=MESH,
            )
        )
        go(p_copy[-1])
    for a, piece in ((0, 2), (1, 0), (1, 1), (1, 2)):
        send_weights(a, piece)

    for d in range(1, 8):
        router_rows(d, True).wait_recv()
    rgf[...] = rg[...].reshape(2048, 128).astype(F32)
    for k in range(16):
        rfull[:, 128 * k : 128 * k + 128] = rgf[pl.ds(k, 128, stride=16), :].astype(BF)

    for copy in p_copy:
        copy.wait_recv()
    hidden = residual[...].reshape(TOK, D).astype(F32) + part[y]
    for d in range(3):
        hidden = hidden + precv[d].astype(F32)
    hid[...] = hidden
    scale = lax.rsqrt(jnp.mean(hidden * hidden, -1, keepdims=True) + 1e-06)
    normed = (hidden * scale * gain[...]).astype(BF)
    tok[0] = normed
    scores = lax.dot_general(rfull[...], normed, NT, preferred_element_type=F32)
    scores = scores.astype(BF).astype(F32)
    id_rows = ids[...].reshape(TOK, TOPK)
    expert_lane = lax.broadcasted_iota(jnp.int32, (TOK, 128), 1)
    named = expert_lane == id_rows[:, 0:1]
    for k in range(1, TOPK):
        named = named | (expert_lane == id_rows[:, k : k + 1])
    hits = jnp.where(named, 1.0, 0.0).T
    named = hits > 0.0
    top = jnp.max(jnp.where(named, scores, -3e38), 0, keepdims=True)
    grown = jnp.where(named, jnp.exp(jnp.minimum(scores - top, 0.0)), 0.0)
    mix = grown / jnp.sum(grown, 0, keepdims=True)
    before = lax.broadcasted_iota(jnp.int32, (TOK, TOK), 0) < lax.broadcasted_iota(
        jnp.int32, (TOK, TOK), 1
    )
    rank = jnp.dot(
        hits.astype(BF), jnp.where(before, 1.0, 0.0).astype(BF), preferred_element_type=F32
    )
    code = jnp.where(named, 2.0 * rank + mix, -1.0)
    for k in range(4):
        met[0, :, 32 * k : 32 * k + 32] = code[32 * k : 32 * k + 32, :]

    tok_copy, met_copy = {}, {}
    for dr in range(2):
        for k in range(1, 9):
            src = 0 if k == 1 else slot_of(dr, k - 1)
            dst = slot_of(dr, k)
            for chunk in range(4):
                if k == 8 and chunk // 2 != dr:
                    continue
                rows, cols = pl.ds(16 * (chunk // 2), 16), pl.ds(1024 * (chunk % 2), 1024)
                tok_copy[dr, k, chunk] = pltpu.make_async_remote_copy(
                    src_ref=tok.at[src, rows, cols],
                    dst_ref=tok.at[dst, rows, cols],
                    send_sem=tok_s.at[dr, k - 1, chunk],
                    recv_sem=tok_r.at[dr, k - 1, chunk],
                    device_id=z_next[dr],
                    device_id_type=MESH,
                )
            if k < 8 or dr == 0:
                met_copy[dr, k] = pltpu.make_async_remote_copy(
                    src_ref=met.at[src],
                    dst_ref=met.at[dst],
                    send_sem=met_s.at[dr, k - 1],
                    recv_sem=met_r.at[dr, k - 1],
                    device_id=z_next[dr],
                    device_id_type=MESH,
                )

    for dr in range(2):
        go(met_copy[dr, 1])
    for chunk in range(4):
        for dr in range(2):
            go(tok_copy[dr, 1, chunk])
    pass_on(0)

    row = lax.broadcasted_iota(jnp.int32, (128, 128), 0)
    lane = lax.broadcasted_iota(jnp.int32, (128, 128), 1)
    row_x, row_c = row // 32, lax.rem(row // 16, 2)
    row_q, row_s = lax.rem(row // 4, 4), lax.rem(row, 4)
    lane_g = lane // 32

    def folded(values):
        total = values
        for k in range(1, 4):
            total = total + pltpu.roll(values, 32 * k, 1)
        return jnp.where(lane_g == row_q, total, 0.0)

    def x_copy(g, d):
        p = lax.rem(me8 + d, 8)
        return pltpu.make_async_remote_copy(
            src_ref=sendx.at[g, p],
            dst_ref=rx.at[g, me8],
            send_sem=x_s.at[g, d],
            recv_sem=x_r.at[g, d],
            device_id=at_slot(p),
            device_id_type=MESH,
        )

    def y_copy(g, d):
        p = lax.rem(me8 + d, 8)
        return pltpu.make_async_remote_copy(
            src_ref=ysend.at[g, p],
            dst_ref=ry.at[g, me8],
            send_sem=y_s.at[g, d],
            recv_sem=y_r.at[g, d],
            device_id=at_source(p),
            device_id_type=MESH,
        )

    def landed(buffer, sems, g, d):
        p = lax.rem(me8 + 8 - d, 8)
        pltpu.make_async_remote_copy(
            src_ref=buffer.at[g, p],
            dst_ref=buffer.at[g, p],
            send_sem=sems.at[g, d],
            recv_sem=sems.at[g, d],
            device_id=at_slot(p),
            device_id_type=MESH,
        ).wait_recv()

    def landed_all(buffer, sems, g):
        for d in range(1, 8):
            landed(buffer, sems, g, d)

        @pl.when(core == 1)
        def _():
            landed(buffer, sems, g, 0)

    def dispatch(g):
        held = {}

        def select():
            value = jnp.full((128, 128), -1.0, F32)
            for q in range(4):
                for c in range(2):
                    line = met[4 * g + q, pl.ds(2 * z + lax.rem(y + c, 2), 1), :]
                    value = jnp.where((row_q == q) & (row_c == c), line, value)
            rank_here = (
                jnp.where(value >= 2.0, 1.0, 0.0)
                + jnp.where(value >= 4.0, 1.0, 0.0)
                + jnp.where(value >= 6.0, 1.0, 0.0)
            )
            picked = (value >= 0.0) & (lane_g == row_x) & (rank_here == row_s.astype(F32))
            held["choose"] = folded(jnp.where(picked, 1.0, 0.0)).astype(BF)
            weigh = folded(jnp.where(picked, value - 2.0 * rank_here, 0.0))
            swt[g] = weigh.T.astype(BF)

        def pick(c):
            cols = slice(512 * c, 512 * c + 512)
            rows = tok[4 * g : 4 * g + 4, :, cols].reshape(128, 512)
            sent = jnp.dot(held["choose"], rows, preferred_element_type=F32).astype(BF)
            sendx[g, :, :, cols] = sent.reshape(8, 16, 512)

        def send():
            for d in range(1, 8):
                go(x_copy(g, d))

            @pl.when(core == 1)
            def _():
                x_copy(g, 0).start()

            @pl.when(core == 0)
            def _():
                rx[g, me8] = sendx[g, me8]

        return [select] + [functools.partial(pick, c) for c in range(4)] + [send]

    work = []

    def do_next():
        if work:
            work.pop(0)()

    def do_all():
        while work:
            do_next()

    for k in range(1, 9):
        for chunk in range(4):
            for dr in range(2):
                if chunk == 0 and (dr, k) in met_copy:
                    met_copy[dr, k].wait_recv()
                    if (dr, k + 1) in met_copy:
                        go(met_copy[dr, k + 1])
                if (dr, k, chunk) in tok_copy:
                    tok_copy[dr, k, chunk].wait_recv()
                    if (dr, k + 1, chunk) in tok_copy:
                        go(tok_copy[dr, k + 1, chunk])
            do_next()
        if k % 2 == 0:
            work.extend(dispatch(k // 2 - 1))
        if k == 2:
            work.append(functools.partial(send_weights, 2, 0))
        if k == 5:
            work.append(functools.partial(send_weights, 2, 1))
        if k == 6:
            work.append(functools.partial(pass_on, 1))
    do_all()

    send_weights(2, 2)

    def hidden_units(slot, h):
        rows = rx[2 * h : 2 * h + 2].reshape(256, D)
        gate_pre = lax.dot_general(rows, wb[slot, 0:192], NT, preferred_element_type=F32)
        up_pre = lax.dot_general(rows, wb[slot, 192:384], NT, preferred_element_type=F32)
        activated = gate_pre * (1.0 / (1.0 + jnp.exp(-gate_pre))) * up_pre
        act[slot, 256 * h : 256 * h + 256, :] = activated.astype(BF)

    landed_all(rx, x_r, 0)
    landed_all(rx, x_r, 1)
    weight_ready(0)
    weight_ready(1)
    for slot in range(4):
        hidden_units(slot, 0)
    pass_piece(2, 0)
    pass_piece(2, 1)
    landed_all(rx, x_r, 2)
    landed_all(rx, x_r, 3)
    for slot in range(4):
        hidden_units(slot, 1)
    pass_piece(2, 2)
    weight_ready(2)

    def project(g):
        for c in range(4):
            cols = slice(512 * c, 512 * c + 512)
            total = jnp.dot(
                act[0, 128 * g : 128 * g + 128, :],
                wb[0, 384:576, cols],
                preferred_element_type=F32,
            )
            for slot in range(1, 4):
                total = total + jnp.dot(
                    act[slot, 128 * g : 128 * g + 128, :],
                    wb[slot, 384:576, cols],
                    preferred_element_type=F32,
                )
            ysend[g, :, :, cols] = total.astype(BF).reshape(8, 16, 512)
        for d in range(1, 8):
            go(y_copy(g, d))

        @pl.when(core == 1)
        def _():
            y_copy(g, 0).start()

        @pl.when(core == 0)
        def _():
            ry[g, me8] = ysend[g, me8]

    for g in (3, 2, 1, 0):
        project(g)

    def gather_back(g):
        def wait():
            landed_all(ry, y_r, g)

        def weigh(c):
            cols = slice(512 * c, 512 * c + 512)
            rows = ry[g, :, :, cols].reshape(128, 512)
            mixed = jnp.dot(swt[g], rows, preferred_element_type=F32)
            part[4 * g : 4 * g + 4, :, cols] = mixed.reshape(4, 32, 512)

        return [wait] + [functools.partial(weigh, c) for c in range(4)]

    rs_copy = {}
    for dr in range(2):
        for j in range(8):
            for chunk in range(4):
                if j == 0 and chunk // 2 != dr:
                    continue
                rows, cols = pl.ds(16 * (chunk // 2), 16), pl.ds(1024 * (chunk % 2), 1024)
                rs_copy[dr, j, chunk] = pltpu.make_async_remote_copy(
                    src_ref=rss.at[dr, j, rows, cols],
                    dst_ref=rsr.at[dr, j, rows, cols],
                    send_sem=rs_s.at[dr, j, chunk],
                    recv_sem=rs_r.at[dr, j, chunk],
                    device_id=z_next[dr],
                    device_id_type=MESH,
                )

    work.extend(gather_back(3))
    do_all()
    for j in range(8):
        if j in (2, 4, 6):
            do_all()
        if j in (1, 3, 5):
            work.extend([lambda: None] * 2 + gather_back(2 - j // 2))
        for chunk in range(4):
            rows = slice(16 * (chunk // 2), 16 * (chunk // 2) + 16)
            cols = slice(1024 * (chunk % 2), 1024 * (chunk % 2) + 1024)
            for dr in range(2):
                if (dr, j, chunk) not in rs_copy:
                    continue
                total = part[slot_of(1 - dr, 8 - j), rows, cols]
                if (dr, j - 1, chunk) in rs_copy:
                    rs_copy[dr, j - 1, chunk].wait_recv()
                    total = total + rsr[dr, j - 1, rows, cols].astype(F32)
                rss[dr, j, rows, cols] = total.astype(BF)
                go(rs_copy[dr, j, chunk])
            do_next()
    for chunk in range(4):
        rows = slice(16 * (chunk // 2), 16 * (chunk // 2) + 16)
        cols = slice(1024 * (chunk % 2), 1024 * (chunk % 2) + 1024)
        total = hid[rows, cols] + part[0, rows, cols]
        for dr in range(2):
            rs_copy[dr, 7, chunk].wait_recv()
            total = total + rsr[dr, 7, rows, cols].astype(F32)
        out[rows, cols] = total.astype(BF)

    for copy in pending:
        copy.wait_send()

    @pl.when(core == 1)
    def _():
        for g in range(4):
            x_copy(g, 0).wait_send()
            y_copy(g, 0).wait_send()

    @pl.when(keeper)
    def _():
        for a in range(3):
            for half in range(2):
                for piece in range(3):
                    give(2, a, half, piece).wait_send()
            share_weight(a).wait_send()

    @pl.when(jnp.logical_not(keeper))
    def _():
        for a in range(3):
            for half in range(2):
                for piece in range(3):
                    give(0, a, half, piece).wait_send()
                    give(1, a, half, piece).wait_send()


def layer(*operands):
    vmem = pl.BlockSpec(memory_space=pltpu.VMEM)
    anywhere = pl.BlockSpec(memory_space=pl.ANY)
    dma = pltpu.SemaphoreType.DMA
    return pl.pallas_call(
        layer_kernel,
        out_shape=jax.ShapeDtypeStruct((TOK, D), BF),
        in_specs=[vmem] * 3 + [anywhere] * 4 + [vmem] * 3 + [anywhere] * 3,
        out_specs=vmem,
        scratch_shapes=[
            pltpu.VMEM((2, 8, 2, D), BF),
            pltpu.VMEM((TOK, D), BF),
            pltpu.VMEM((TOK, 256), BF),
            pltpu.VMEM((TOK, 256), BF),
            pltpu.VMEM((4, TOK, 512), BF),
            pltpu.VMEM((4, 256, 128), BF),
            pltpu.VMEM((4, 256, 128), BF),
            pltpu.VMEM((4, TOK, 128), BF),
            pltpu.VMEM((4, TOK, 128), BF),
            pltpu.VMEM((4, TOK, 512), BF),
            pltpu.VMEM((512, D), BF),
            pltpu.VMEM((4, TOK, D), BF),
            pltpu.VMEM((3, TOK, D), BF),
            pltpu.VMEM((TOK, D), F32),
            pltpu.VMEM((16, 128), F32),
            pltpu.VMEM((4, ZN, 2, 16, 128), BF),
            pltpu.VMEM((2048, 128), F32),
            pltpu.VMEM((128, D), BF),
            pltpu.VMEM((16, TOK, D), BF),
            pltpu.VMEM((16, TOK, 128), F32),
            pltpu.VMEM((4, 128, 128), BF),
            pltpu.VMEM((4, 8, 16, D), BF),
            pltpu.VMEM((4, 8, 16, D), BF),
            pltpu.VMEM((4, 512, 192), BF),
            pltpu.VMEM((4, 8, 16, D), BF),
            pltpu.VMEM((4, 8, 16, D), BF),
            pltpu.VMEM((16, TOK, D), F32),
            pltpu.VMEM((2, 8, TOK, D), BF),
            pltpu.VMEM((2, 8, TOK, D), BF),
            pltpu.VMEM((4, 576, D), BF),
            dma((3, 5)), dma((3, 5)), dma((7,)),
            dma((3,)), dma((3,)),
            dma((15,)), dma((15,)),
            dma((7,)), dma((7,)),
            dma((2, 8, 4)), dma((2, 8, 4)),
            dma((2, 8)), dma((2, 8)),
            dma((4, 8)), dma((4, 8)),
            dma((4, 8)), dma((4, 8)),
            dma((2, 8, 4)), dma((2, 8, 4)),
            dma((3, 3, 2, 3)), dma((3, 3, 3)),
            dma((3, 3, 3)), dma((3, 3, 3)),
            dma((3,)), dma((3,)),
            dma((3,)),
        ],
        compiler_params=pltpu.CompilerParams(
            collective_id=0, has_side_effects=True, vmem_limit_bytes=56 * 1024 * 1024
        ),
        cost_estimate=pl.CostEstimate(
            flops=2 * 3 * 512 * 2048 * 768, bytes_accessed=8 << 20, transcendentals=512 * 768
        ),
    )(*operands)


def per_device(
    queries,
    block_keys,
    block_values,
    cache_keys,
    cache_values,
    residual,
    out_weight,
    norm_gain,
    router,
    gate_weight,
    up_weight,
    down_weight,
    expert_ids,
):
    block_output = layer(
        queries,
        block_keys,
        block_values,
        cache_keys.reshape(256, 256),
        cache_values.reshape(256, 256),
        residual,
        out_weight,
        norm_gain.reshape(1, D),
        router.T,
        expert_ids,
        gate_weight[0].T,
        up_weight[0].T,
        down_weight[0].T,
    )
    return block_output.reshape(residual.shape)


def solution(mesh):
    in_specs = (
        P("exp", "ctx", None, None),
        P("exp", "ctx", None, None),
        P("exp", "ctx", None, None),
        P("exp", "ctx", None),
        P("exp", "ctx", None),
        P("exp", "ctx", None, None),
        P("ctx", None),
        P(),
        P(None, "exp"),
        P("exp", None, "ctx"),
        P("exp", None, "ctx"),
        P("exp", None, "ctx"),
        P("exp", "ctx", None, None),
    )
    out_specs = P("exp", "ctx", None, None)
    return jax.shard_map(
        per_device, mesh=mesh, in_specs=in_specs, out_specs=out_specs, check_vma=False
    )
```
